512 devices in a mesh: segment: 8 (over y, core), rows: 16 (over z), dp: 4 (over x).
Axes of the slice: x: 4, y: 4, z: 16, core: 2. Of those that a mesh axis runs over, the one named last changes fastest.
Arguments:
- clips: bfloat16 [4, 4, 4, 128, 8, 128], P(None, 'dp', None, 'rows'), may hold values from -80 to 80
- lengths: int32 [4, 4], P(None, 'dp'), may hold values from 1 to 4, as said below
- conv_weight: bfloat16 [8, 3456, 128], P('segment'), may hold values from -0.109375 to 0.109375
- norm_gain: float32 [8, 128], P('segment'), may hold values from 0.5 to 2
- norm_shift: float32 [8, 128], P('segment'), may hold values from -1 to 1
- conv_bias: float32 [8, 128], P('segment'), may hold values from -3 to 3
- cotangent: bfloat16 [8, 4, 4, 4, 128, 8, 128], P('segment', None, 'dp', None, 'rows'), may hold values from -6 to 6
Outputs:
- stash: bfloat16 [8, 4, 4, 4, 128, 8, 128], P('segment', None, 'dp', None, 'rows')
- weight_grad: float32 [8, 3456, 128], P('segment')
The draws below stay inside these ranges and needn't reach their ends.
Inputs may be any that keep to these rules, and one draw needn't show every extreme that they name: lengths[m, clip] real frames lead each clip; the frames after them are padding; some clip has all 4 frames.
All inputs are finite; a program needn't handle non-finite values.
Results may differ from the reference program's by a relative error of at most 0.009.
Values may be sent and summed in bfloat16 or wider, within the bound.
A program may use at most 64 MiB of HBM per device.

```python
import math
import jax
import jax.numpy as jnp
from jax import lax

C = 128
GROUPS = 32
MB = 4
FRAMES = 4
COLS = 8
SEGMENTS = 8
CLIPS = 4
HEIGHT = 128


def draw_clips(key, part):
    keys = jax.random.split(key, 3)
    place = jnp.arange(HEIGHT, dtype=jnp.float32) / max(HEIGHT - 1, 1)
    shape = (MB, CLIPS, FRAMES, HEIGHT, COLS, C)
    rise = jnp.exp(jnp.log(3.0) * place)
    noise = jnp.clip(jax.random.normal(keys[0], shape, jnp.float32), -5.0, 5.0)
    chan = jnp.exp(jax.random.uniform(keys[1], (C,), jnp.float32, jnp.log(0.5), jnp.log(2.0)))
    offset = jnp.clip(0.5 * jax.random.normal(keys[2], (MB, CLIPS, 1, 1, 1, C), jnp.float32), -1.0, 1.0)
    return (rise[None, None, None, :, None, None] * (offset + chan * noise)).astype(jnp.bfloat16)


def draw_lengths(key, part):
    first, second = jax.random.split(key)
    counts = jax.random.randint(first, (MB * CLIPS,), 1, FRAMES + 1)
    full_at = jax.random.randint(second, (), 0, MB * CLIPS)
    counts = jnp.where(jnp.arange(MB * CLIPS) == full_at, FRAMES, counts)
    return counts.reshape(MB, CLIPS).astype(jnp.int32)


def block_levels(rng, shape, cuts, least, top_value):
    def one(dim, shards_of):
        steps = jax.random.uniform(jax.random.fold_in(jax.random.fold_in(rng, 6), dim), (shards_of,), jnp.float32, least / len(cuts), top_value / len(cuts))
        return jnp.repeat(jnp.exp(steps), shape[dim] // shards_of).reshape((-1,) + (1,) * (len(shape) - dim - 1))

    factor_of = one(*cuts[0])
    for cut in cuts[1:]:
        factor_of = factor_of * one(*cut)
    return factor_of


def centred(rng, extent, deviation, most, cuts=(), kind=jnp.bfloat16):
    factor_of = block_levels(rng, extent, cuts, -0.22, 0.18) if cuts else 1.0
    drawn = jax.random.normal(rng, extent, jnp.float32) * deviation * factor_of
    return jnp.minimum(jnp.maximum(drawn, -most), most).astype(kind)


def setup_inputs(seed: int = 0) -> dict:
    key_list = jax.random.split(jax.random.key(seed), 8)
    return {
        "clips": draw_clips(jax.random.fold_in(key_list[7], 71), 0),
        "lengths": draw_lengths(jax.random.fold_in(key_list[7], 71), 0),
        "conv_weight": centred(key_list[2], (SEGMENTS, 27 * C, C), (27 * C) ** -0.5, 0.109375, ((0, 8),)),
        "norm_gain": jnp.clip(jnp.exp(math.log(2.0) - 1.3862944 * jax.random.uniform(key_list[3], (SEGMENTS, C), jnp.float32) ** block_levels(key_list[3], (SEGMENTS, C), ((0, 8),), -0.2, 0.2)), 0.5, 2.0),
        "norm_shift": jnp.clip(jax.random.uniform(key_list[4], (SEGMENTS, C), jnp.float32, -1.0, 1.0) * block_levels(key_list[4], (SEGMENTS, C), ((0, 8),), -0.4, 0.0), -1.0, 1.0),
        "conv_bias": centred(key_list[5], (SEGMENTS, C), 0.5, 3.0, ((0, 8),), jnp.float32),
        "cotangent": centred(key_list[6], (SEGMENTS, MB, CLIPS, FRAMES, HEIGHT, COLS, C), 1.0, 6.0, ((0, 8), (2, 4), (4, 16))),
    }


eps = 1e-06

def block(inputs, length, weight, gain, shift, bias):
    clip_count, frames, height, cols, chans = inputs.shape
    sub = chans // GROUPS
    values = inputs.astype(jnp.float32)
    mask = (jnp.arange(frames)[None, :] < length[:, None]).astype(jnp.float32)
    mask_six = mask[:, :, None, None, None, None]
    grouped = values.reshape(clip_count, frames, height, cols, GROUPS, sub)
    count = (length * (height * cols * sub)).astype(jnp.float32)[:, None]
    mean = lax.optimization_barrier(jnp.sum(grouped * mask_six, axis=(1, 2, 3, 5))) / count
    centered = grouped - mean[:, None, None, None, :, None]
    var = lax.optimization_barrier(jnp.sum(centered * centered * mask_six, axis=(1, 2, 3, 5))) / count
    rstd = lax.rsqrt(var + eps)
    normed = (centered * rstd[:, None, None, None, :, None]).reshape(values.shape) * gain + shift
    hidden = jax.nn.silu(normed).astype(jnp.bfloat16)
    padded = jnp.pad(hidden, ((0, 0), (0, 0), (1, 1), (1, 1), (0, 0)))
    padded = jnp.concatenate([padded[:, :1], padded[:, :1], padded], axis=1)
    pieces = []
    for tap_t in range(3):
        for tap_h in range(3):
            for tap_w in range(3):
                pieces.append(padded[:, tap_t:tap_t + frames, tap_h:tap_h + height, tap_w:tap_w + cols, :])
    patches = jnp.concatenate(pieces, axis=-1).reshape(-1, 27 * chans)
    conv = jnp.dot(patches, weight, preferred_element_type=jnp.float32).reshape(values.shape)
    mask_five = mask[:, :, None, None, None]
    result = ((values + conv + bias) * mask_five).astype(jnp.bfloat16)
    return (result, patches, mask_five.astype(jnp.bfloat16))

def reference(clips, lengths, conv_weight, norm_gain, norm_shift, conv_bias, cotangent):
    scale = 1.0 / math.sqrt(MB * CLIPS * FRAMES * HEIGHT * COLS)

    def one_batch(grads, inputs):
        current, length, cot = inputs
        outputs = []
        updated = []
        for segment in range(SEGMENTS):
            current, patches, mask_five = block(current, length, conv_weight[segment], norm_gain[segment], norm_shift[segment], conv_bias[segment])
            outputs.append(current)
            masked = (cot[segment] * mask_five).reshape(-1, C)
            term = lax.dot_general(patches, masked, (((0,), (0,)), ((), ())), preferred_element_type=jnp.float32)
            updated.append(grads[segment] + term)
        return (jnp.stack(updated), jnp.stack(outputs))
    start = jnp.zeros((SEGMENTS, 27 * C, C), jnp.float32)
    grads, stash = lax.scan(one_batch, start, (clips, lengths, jnp.moveaxis(cotangent, 1, 0)))
    return (jnp.moveaxis(stash, 0, 1), grads * scale)
```

```python
import math

import jax
import jax.numpy as jnp
from jax import lax
from jax.experimental import pallas as pl
from jax.experimental.pallas import tpu as pltpu
from jax.sharding import PartitionSpec as P

MESH = pl.DeviceIdType.MESH
EPS = 1e-06
SEGS, ZS, XS, MB, FR, C = 8, 16, 4, 4, 4, 128
WIN = 4
ROWS = 32
CELLS = ROWS * 8
PIECES, PROWS = 14, 64
QROWS = 864
F32, BF16 = jnp.float32, jnp.bfloat16


def group_sum(v):
    lane = lax.broadcasted_iota(jnp.int32, v.shape, 1)
    v = v + jnp.where(lane % 2 == 0, pltpu.roll(v, 127, 1), pltpu.roll(v, 1, 1))
    return v + jnp.where(lane % 4 < 2, pltpu.roll(v, 126, 1), pltpu.roll(v, 2, 1))


def kernel(clips, lengths, w, gain, shift, bias, cot, stash, grad,
           xin, xout, halo, wcat, hs, cotz, rhs, acc, part, xr, zs, zr, st_out, st_in,
           w_sem, cg_s, cg_r, ct_s, ct_r, ss_s, ss_r, rl_s, rl_r, hl_s, hl_r, st_s, st_r,
           xs_s, xs_r, zs_s, zs_r, ag_s, ag_r, xg_s, xg_r):
    seg = lax.axis_index("segment")
    z = lax.axis_index("rows")
    x = lax.axis_index("dp")
    m = z // WIN
    k = z % WIN
    nxt = lax.rem(seg + 1, SEGS)
    prv = lax.rem(seg + SEGS - 1, SEGS)
    first = seg == 0
    last = seg == SEGS - 1

    def dev(s, zz, xx):
        return {"segment": s, "rows": zz, "dp": xx}

    def remote(src, dst, ssem, rsem, target):
        return pltpu.make_async_remote_copy(
            src_ref=src, dst_ref=dst, send_sem=ssem, recv_sem=rsem, device_id=target, device_id_type=MESH)

    def arrived(ref, sem):
        pltpu.make_async_copy(ref, ref, sem).wait()

    w_copies = [
        pltpu.make_async_copy(w.at[pl.ds(a * 9 * C, 9 * C)], wcat.at[:, pl.ds(a * C, C)], w_sem.at[a])
        for a in range(3)
    ]
    for cp in w_copies:
        cp.start()

    bar = pltpu.get_barrier_semaphore()

    def greet(target):
        pl.semaphore_signal(bar, inc=1, device_id=target, device_id_type=MESH)

    for o in range(1, ZS):
        greet(dev(seg, lax.rem(z + o, ZS), x))
    for o in range(1, XS):
        greet(dev(seg, z, lax.rem(x + o, XS)))
    for kk in range(WIN):
        greet(dev(nxt, m * WIN + kk, x))
        greet(dev(prv, m * WIN + kk, x))
    pl.semaphore_wait(bar, ZS - 1 + XS - 1 + 2 * WIN)

    def regroup(src, dst, ssem, rsem):
        for i in range(MB):
            to = i * WIN + m
            here = dst.at[:, pl.ds(pl.multiple_of(k * 64, 64), 64)]

            @pl.when(to != z)
            def _():
                remote(src.at[i], here, ssem.at[i], rsem.at[k], dev(seg, to, x)).start()

            @pl.when(to == z)
            def _():
                pltpu.make_async_copy(src.at[i], here, rsem.at[k]).start()

    def regroup_recv(dst, rsem):
        for j in range(WIN):
            arrived(dst.at[:, pl.ds(j * 64, 64)], rsem.at[j])

    def regroup_sent(src, ssem):
        for i in range(MB):
            @pl.when(i * WIN + m != z)
            def _():
                arrived(src.at[i], ssem.at[i])

    length = lengths[m, 0]
    mask = [jnp.where(f < length, 1.0, 0.0).astype(F32) for f in range(FR)]
    n_dev = (length * CELLS).astype(F32)

    def local_sums(ref):
        total = jnp.zeros((8, C), F32)
        for f in range(FR):
            v = ref[f].astype(F32).reshape(ROWS, 8, C)
            total = total + jnp.sum(v, axis=0) * mask[f]
        return jnp.broadcast_to(jnp.sum(total, axis=0, keepdims=True), (8, C))

    def local_stats(ref):
        sums = local_sums(ref)
        mean = (sums / n_dev)[None]
        total = jnp.zeros((8, C), F32)
        for f in range(FR):
            v = ref[f].astype(F32).reshape(ROWS, 8, C) - mean
            total = total + jnp.sum(v * v, axis=0) * mask[f]
        st_out[0] = sums
        st_out[1] = jnp.broadcast_to(jnp.sum(total, axis=0, keepdims=True), (8, C))

    def edge_copies(ref, to):
        up = remote(ref.at[:, pl.ds(0, 16)], halo.at[1], hl_s.at[0], hl_r.at[1], dev(to, z - 1, x))
        down = remote(ref.at[:, pl.ds(CELLS - 16, 16)], halo.at[0], hl_s.at[1], hl_r.at[0], dev(to, z + 1, x))
        return up, down

    def send_edges(ref, to):
        @pl.when(k > 0)
        def _():
            edge_copies(ref, to)[0].start()

        @pl.when(k < WIN - 1)
        def _():
            edge_copies(ref, to)[1].start()

    def edges_sent(ref):
        @pl.when(k > 0)
        def _():
            arrived(ref.at[:, pl.ds(0, 16)], hl_s.at[0])

        @pl.when(k < WIN - 1)
        def _():
            arrived(ref.at[:, pl.ds(CELLS - 16, 16)], hl_s.at[1])

    @pl.when(k == 0)
    def _():
        halo[0] = jnp.zeros((FR, 16, C), BF16)

    @pl.when(k == WIN - 1)
    def _():
        halo[1] = jnp.zeros((FR, 16, C), BF16)

    @pl.when(first)
    def _():
        regroup(clips, xin, cg_s, cg_r)
        regroup_recv(xin, cg_r)
        send_edges(xin, seg)
        local_stats(xin)
        for o in range(1, WIN):
            remote(st_out, st_in.at[k], st_s.at[o], st_r.at[k], dev(seg, m * WIN + lax.rem(k + o, WIN), x)).start()
        st_in[k] = st_out[...]
        regroup_sent(clips, cg_s)
        for o in range(1, WIN):
            arrived(st_out, st_s.at[o])
        edges_sent(xin)

    @pl.when(seg > 1)
    def _():
        regroup(cot, cotz, ct_s, ct_r)

    @pl.when(seg > 0)
    def _():
        for h in range(2):
            arrived(xin.at[:, pl.ds(h * 128, 128)], rl_r.at[h])

    @pl.when(seg <= 1)
    def _():
        regroup(cot, cotz, ct_s, ct_r)

    @pl.when(k > 0)
    def _():
        arrived(halo.at[0], hl_r.at[0])

    @pl.when(k < WIN - 1)
    def _():
        arrived(halo.at[1], hl_r.at[1])

    for kk in range(WIN):
        @pl.when(jnp.logical_or(seg > 0, k != kk))
        def _():
            arrived(st_in.at[kk], st_r.at[kk])

    total = st_in[0, 0] + st_in[1, 0] + st_in[2, 0] + st_in[3, 0]
    count = n_dev * (4.0 * WIN)
    mean = group_sum(total) / count
    spread = jnp.zeros((8, C), F32)
    for kk in range(WIN):
        off = st_in[kk, 0] / n_dev - mean
        spread = spread + st_in[kk, 1] + n_dev * (off * off)
    rstd = lax.rsqrt(group_sum(spread) / count + EPS)
    scale = rstd * gain[...]
    offset = jnp.broadcast_to(shift[...], (8, C))
    col = lax.broadcasted_iota(jnp.int32, (1, 8, C), 1)

    def act(v):
        v = (v - mean[None]) * scale[None] + offset[None]
        return v / (1.0 + jnp.exp(-v))

    def put(row, n, per_frame):
        for fp in range(2):
            pair = [per_frame[2 * fp], per_frame[2 * fp + 1]]
            for d in range(3):
                if d == 0:
                    out = [jnp.where(col == 0, 0.0, pltpu.roll(h.reshape(n * 8, C), 1, 0).reshape(n, 8, C)) for h in pair]
                elif d == 2:
                    out = [jnp.where(col == 7, 0.0, pltpu.roll(h.reshape(n * 8, C), n * 8 - 1, 0).reshape(n, 8, C)) for h in pair]
                else:
                    out = pair
                hs[d, pl.ds(row, n), fp] = jnp.concatenate(out, axis=1).astype(BF16)

    top_here, bottom_here = k > 0, k < WIN - 1
    put(0, 1, [jnp.where(top_here, act(halo[0, f, 8:16].astype(F32).reshape(1, 8, C)), 0.0) for f in range(FR)])
    put(ROWS + 1, 1, [jnp.where(bottom_here, act(halo[1, f, 0:8].astype(F32).reshape(1, 8, C)), 0.0) for f in range(FR)])

    def norm_step(j, c):
        put(8 * j + 1, 8, [
            act(xin[f, pl.ds(pl.multiple_of(j * 64, 64), 64)].astype(F32).reshape(8, 8, C)) for f in range(FR)])
        return c

    lax.fori_loop(0, ROWS // 8, norm_step, 0)

    for cp in w_copies:
        cp.wait()

    bias_row = bias[...].reshape(1, 1, C)
    half = ROWS // 2
    for h in range(2):
        def taps(fp):
            return jnp.concatenate(
                [hs[d, pl.ds(h * half + b, half), fp].reshape(half * 16, C) for b in range(3) for d in range(3)], axis=1)

        p01 = jnp.dot(taps(0), wcat[...], preferred_element_type=F32).reshape(half, 2, 8, 3 * C)
        p23 = jnp.dot(taps(1), wcat[:, C:], preferred_element_type=F32).reshape(half, 2, 8, 2 * C)
        a0, a1, a2 = slice(0, C), slice(C, 2 * C), slice(2 * C, 3 * C)
        early = p01[:, 0, :, a0] + p01[:, 0, :, a1]
        outs = [
            early + p01[:, 0, :, a2],
            early + p01[:, 1, :, a2],
            p01[:, 0, :, a0] + p01[:, 1, :, a1] + p23[:, 0, :, a1],
            p01[:, 1, :, a0] + p23[:, 0, :, a0] + p23[:, 1, :, a1],
        ]
        for f in range(FR):
            v = xin[f, h * 128:(h + 1) * 128].astype(F32).reshape(half, 8, C)
            out = (v + outs[f] + bias_row) * mask[f]
            xout[f, h * 128:(h + 1) * 128] = out.reshape(128, C).astype(BF16)

        @pl.when(jnp.logical_not(last))
        def _():
            part_h = (slice(None), pl.ds(h * 128, 128))
            remote(xout.at[part_h], xin.at[part_h], rl_s.at[h], rl_r.at[h], dev(nxt, z, x)).start()

    @pl.when(jnp.logical_not(last))
    def _():
        send_edges(xout, nxt)
        local_stats(xout)
        for kk in range(WIN):
            remote(st_out, st_in.at[k], st_s.at[kk], st_r.at[k], dev(nxt, m * WIN + kk, x)).start()

    for j in range(WIN):
        to = k * WIN + j
        src = xout.at[:, pl.ds(j * 64, 64)]

        @pl.when(to != z)
        def _():
            remote(src, stash.at[m], ss_s.at[j], ss_r.at[m], dev(seg, to, x)).start()

        @pl.when(to == z)
        def _():
            pltpu.make_async_copy(src, stash.at[m], ss_r.at[m]).start()

    regroup_recv(cotz, ct_r)

    def rhs_step(j, c):
        cut = pl.ds(pl.multiple_of(j * 64, 64), 64)
        cs = [cotz[f, cut].astype(F32).reshape(8, 8, C) * mask[f] for f in range(FR)]
        zero = jnp.zeros((8, 8, C), F32)
        two = cs[0] + cs[1]
        cols = [
            [[two + cs[2], cs[3]], [zero, zero]],
            [[two, cs[2]], [cs[3], zero]],
            [[cs[0], cs[1]], [cs[2], cs[3]]],
        ]
        for a in range(3):
            for fp in range(2):
                rhs[pl.ds(8 * j, 8), fp, :, a * C:(a + 1) * C] = jnp.concatenate(cols[a][fp], axis=1).astype(BF16)
        return c

    lax.fori_loop(0, ROWS // 8, rhs_step, 0)
    factor = 1.0 / math.sqrt(MB * XS * FR * 128 * 8)
    for b in range(3):
        lhs = jnp.concatenate([hs[d, b:b + ROWS].reshape(ROWS * 32, C) for d in range(3)], axis=1)
        acc[b * 3 * C:(b + 1) * 3 * C] = lax.dot_general(
            lhs, rhs[...].reshape(ROWS * 32, 3 * C), (((0,), (0,)), ((), ())), preferred_element_type=F32)
    for blk in range(12):
        a, i = blk // 4, blk % 4
        part[blk // 3, (blk % 3) * 288:(blk % 3 + 1) * 288] = (
            acc[i * 288:(i + 1) * 288, a * C:(a + 1) * C] * factor).astype(BF16)
    for q in range(4):
        part[q, QROWS:] = jnp.zeros((PIECES * PROWS - QROWS, C), BF16)

    for o in (2, 1, 3):
        to = lax.rem(x + o, XS)
        remote(part.at[to], xr.at[o - 1], xs_s.at[o - 1], xs_r.at[o - 1], dev(seg, z, to)).start()
    for o in (1, 3, 2):
        arrived(xr.at[o - 1], xs_r.at[o - 1])

    def x_sum(p, c):
        cut = pl.ds(pl.multiple_of(p * PROWS, PROWS), PROWS)
        v = part[x, cut].astype(F32)
        for o in range(3):
            v = v + xr[o, cut].astype(F32)
        zs[p] = v.astype(BF16)
        return c

    lax.fori_loop(0, PIECES, x_sum, 0)

    order = (8, 7, 9, 6, 10, 5, 11, 4, 12, 3, 13, 2, 14, 1, 15)
    for o in order:
        to = lax.rem(z + o, ZS)

        @pl.when(to < PIECES)
        def _():
            remote(zs.at[to], zr.at[o - 1], zs_s.at[o - 1], zs_r.at[o - 1], dev(seg, to, x)).start()

    @pl.when(z < PIECES)
    def _():
        v = zs[z].astype(F32)
        for o in order[::-1]:
            arrived(zr.at[o - 1], zs_r.at[o - 1])
            v = v + zr[o - 1].astype(F32)
        grad[x, z] = v.astype(BF16)
        for o in order:
            remote(grad.at[x, z], grad.at[x, z], ag_s.at[o - 1], ag_r.at[o - 1], dev(seg, lax.rem(z + o, ZS), x)).start()

    for o in order[::-1]:
        src_z = lax.rem(z + ZS - o, ZS)

        @pl.when(src_z < PIECES)
        def _():
            arrived(grad.at[x, src_z], ag_r.at[o - 1])

    for o in (2, 1, 3):
        remote(grad.at[x], grad.at[x], xg_s.at[o - 1], xg_r.at[o - 1], dev(seg, z, lax.rem(x + o, XS))).start()

    for j in range(MB):
        arrived(stash.at[j], ss_r.at[j])
    for j in range(WIN):
        @pl.when(k * WIN + j != z)
        def _():
            arrived(xout.at[:, pl.ds(j * 64, 64)], ss_s.at[j])

    regroup_sent(cot, ct_s)

    @pl.when(jnp.logical_not(last))
    def _():
        for h in range(2):
            arrived(xout.at[:, pl.ds(h * 128, 128)], rl_s.at[h])
        for kk in range(WIN):
            arrived(st_out, st_s.at[kk])
        edges_sent(xout)

    for o in range(1, XS):
        arrived(part.at[0], xs_s.at[o - 1])
    for o in range(1, ZS):
        @pl.when(lax.rem(z + o, ZS) < PIECES)
        def _():
            arrived(zs.at[0], zs_s.at[o - 1])

    @pl.when(z < PIECES)
    def _():
        for o in range(1, ZS):
            arrived(zr.at[0], ag_s.at[o - 1])

    for o in range(1, XS):
        arrived(grad.at[lax.rem(x + XS - o, XS)], xg_r.at[o - 1])
        arrived(grad.at[x], xg_s.at[o - 1])


def per_device(clips, lengths, conv_weight, norm_gain, norm_shift, conv_bias, cotangent):
    vmem, anyspace = pltpu.VMEM, pl.ANY
    dma = pltpu.SemaphoreType.DMA
    stash, grad = pl.pallas_call(
        kernel,
        out_shape=(
            jax.ShapeDtypeStruct((MB, FR, 64, C), BF16),
            jax.ShapeDtypeStruct((XS, PIECES, PROWS, C), BF16),
        ),
        in_specs=[
            pl.BlockSpec(memory_space=vmem),
            pl.BlockSpec(memory_space=pltpu.SMEM),
            pl.BlockSpec(memory_space=anyspace),
            pl.BlockSpec(memory_space=vmem),
            pl.BlockSpec(memory_space=vmem),
            pl.BlockSpec(memory_space=vmem),
            pl.BlockSpec(memory_space=vmem),
        ],
        out_specs=(pl.BlockSpec(memory_space=vmem), pl.BlockSpec(memory_space=vmem)),
        scratch_shapes=[
            vmem((FR, CELLS, C), BF16),
            vmem((FR, CELLS, C), BF16),
            vmem((2, FR, 16, C), BF16),
            vmem((9 * C, 3 * C), BF16),
            vmem((3, ROWS + 2, 2, 16, C), BF16),
            vmem((FR, CELLS, C), BF16),
            vmem((ROWS, 2, 16, 3 * C), BF16),
            vmem((9 * C, 3 * C), F32),
            vmem((XS, PIECES * PROWS, C), BF16),
            vmem((XS - 1, PIECES * PROWS, C), BF16),
            vmem((PIECES, PROWS, C), BF16),
            vmem((ZS - 1, PROWS, C), BF16),
            vmem((2, 8, C), F32),
            vmem((WIN, 2, 8, C), F32),
            dma((3,)),
            dma((4,)), dma((4,)), dma((4,)), dma((4,)), dma((4,)), dma((4,)),
            dma((2,)), dma((2,)), dma((2,)), dma((2,)), dma((4,)), dma((4,)),
            dma((3,)), dma((3,)), dma((15,)), dma((15,)), dma((15,)), dma((15,)), dma((3,)), dma((3,)),
        ],
        compiler_params=pltpu.CompilerParams(
            collective_id=0, has_side_effects=True, vmem_limit_bytes=48 * 2**20),
        cost_estimate=pl.CostEstimate(flops=2 * 10**9, bytes_accessed=4 * 10**6, transcendentals=10**6),
    )(
        clips.reshape(MB, FR, 64, C), lengths, conv_weight[0], norm_gain, norm_shift, conv_bias,
        cotangent.reshape(MB, FR, 64, C))
    grads = grad.reshape(XS, PIECES * PROWS, C)[:, :QROWS].reshape(27 * C, C).astype(F32)
    return stash.reshape(1, MB, 1, FR, 8, 8, C), grads[None]


def solution(mesh):
    in_specs = (
        P(None, "dp", None, "rows", None, None),
        P(None, "dp"),
        P("segment", None, None),
        P("segment", None),
        P("segment", None),
        P("segment", None),
        P("segment", None, "dp", None, "rows", None, None),
    )
    out_specs = (P("segment", None, "dp", None, "rows", None, None), P("segment", None, None))
    return jax.shard_map(per_device, mesh=mesh, in_specs=in_specs, out_specs=out_specs, check_vma=False)
```

```python
import math

import jax
import jax.numpy as jnp
from jax import lax
from jax.experimental import pallas as pl
from jax.experimental.pallas import tpu as pltpu
from jax.sharding import PartitionSpec as P

MESH = pl.DeviceIdType.MESH
EPS = 1e-06
SEGS, ZS, XS, MB, FR, C = 8, 16, 4, 4, 4, 128
WIN = 4
ROWS = 32
CELLS = ROWS * 8
CH, PC, PR = 3, 9, 32
F32, BF16 = jnp.float32, jnp.bfloat16


def group_sum(v):
    lane = lax.broadcasted_iota(jnp.int32, v.shape, 1)
    v = v + jnp.where(lane % 2 == 0, pltpu.roll(v, 127, 1), pltpu.roll(v, 1, 1))
    return v + jnp.where(lane % 4 < 2, pltpu.roll(v, 126, 1), pltpu.roll(v, 2, 1))


def kernel(clips_any, lengths_any, w, gain_any, shift_any, bias_any, cot, stash, grad,
           clips, lengths, gain, shift, bias,
           xin, xout, halo, wcat, hs, cotz, rhs, part, xr, zs, zr, st_out, st_in, st_clip, norm, go,
           in_sem, w_sem, cg_s, cg_r, ct_s, ct_r, ss_s, ss_r, rl_s, rl_r, hl_s, hl_r, st_s, st_r,
           sc_s, sc_r,
           xs_s, xs_r, zs_s, zs_r, ag_s, ag_r, xg_s, xg_r):
    seg = lax.axis_index("segment")
    z = lax.axis_index("rows")
    x = lax.axis_index("dp")
    m = z // WIN
    k = z % WIN
    nxt = lax.rem(seg + 1, SEGS)
    prv = lax.rem(seg + SEGS - 1, SEGS)
    first = seg == 0
    last = seg == SEGS - 1

    def dev(s, zz, xx):
        return {"segment": s, "rows": zz, "dp": xx}

    def remote(src, dst, ssem, rsem, target):
        return pltpu.make_async_remote_copy(
            src_ref=src, dst_ref=dst, send_sem=ssem, recv_sem=rsem, device_id=target, device_id_type=MESH)

    def arrived(ref, sem):
        pltpu.make_async_copy(ref, ref, sem).wait()

    in_copies = [
        pltpu.make_async_copy(src, dst, in_sem.at[i])
        for i, (src, dst) in enumerate([
            (clips_any, clips), (lengths_any, lengths), (gain_any, gain), (shift_any, shift), (bias_any, bias)])
    ]
    for cp in in_copies:
        cp.start()

    w_copies = [
        pltpu.make_async_copy(w.at[pl.ds(a * 9 * C, 9 * C)], wcat.at[:, pl.ds(a * C, C)], w_sem.at[a])
        for a in range(3)
    ]
    for cp in w_copies:
        cp.start()

    bar = pltpu.get_barrier_semaphore()

    def greet(target):
        pl.semaphore_signal(bar, inc=1, device_id=target, device_id_type=MESH)

    for o in range(1, ZS):
        greet(dev(seg, lax.rem(z + o, ZS), x))
    for o in range(1, XS):
        greet(dev(seg, z, lax.rem(x + o, XS)))
    for kk in range(WIN):
        greet(dev(nxt, m * WIN + kk, x))
        greet(dev(prv, m * WIN + kk, x))
    for cp in in_copies:
        cp.wait()
    pl.semaphore_wait(bar, ZS - 1 + XS - 1 + 2 * WIN)

    def regroup(src, dst, ssem, rsem):
        for i in range(MB):
            to = i * WIN + m
            here = dst.at[:, pl.ds(pl.multiple_of(k * 64, 64), 64)]

            @pl.when(to != z)
            def _():
                remote(src.at[i], here, ssem.at[i], rsem.at[k], dev(seg, to, x)).start()

            @pl.when(to == z)
            def _():
                pltpu.make_async_copy(src.at[i], here, rsem.at[k]).start()

    def regroup_recv(dst, rsem):
        for j in range(WIN):
            arrived(dst.at[:, pl.ds(j * 64, 64)], rsem.at[j])

    def regroup_sent(src, ssem):
        for i in range(MB):
            @pl.when(i * WIN + m != z)
            def _():
                arrived(src.at[i], ssem.at[i])

    length = lengths[m, 0]
    mask = [jnp.where(f < length, 1.0, 0.0).astype(F32) for f in range(FR)]
    n_dev = (length * CELLS).astype(F32)

    def stats_of(ref, rows, masks, n):
        def over(fn):
            total = jnp.zeros((8, C), F32)
            for f in range(FR):
                total = total + jnp.sum(fn(ref[f].astype(F32).reshape(rows, 8, C)), axis=0) * masks[f]
            return jnp.broadcast_to(jnp.sum(total, axis=0, keepdims=True), (8, C))

        sums = over(lambda v: v)
        mean = (sums / n)[None]
        return sums, over(lambda v: (v - mean) * (v - mean))

    def combine(parts, n):
        count = n * (4.0 * len(parts))
        total = parts[0][0]
        for sums, _ in parts[1:]:
            total = total + sums
        mean = group_sum(total) / count
        spread = jnp.zeros((8, C), F32)
        for sums, squares in parts:
            off = sums / n - mean
            spread = spread + squares + n * (off * off)
        norm[0] = mean
        norm[1] = lax.rsqrt(group_sum(spread) / count + EPS)

    def send_edges(ref, to):
        @pl.when(k > 0)
        def _():
            remote(ref.at[:, pl.ds(0, 16)], halo.at[1], hl_s.at[0], hl_r.at[1], dev(to, z - 1, x)).start()

        @pl.when(k < WIN - 1)
        def _():
            remote(ref.at[:, pl.ds(CELLS - 16, 16)], halo.at[0], hl_s.at[1], hl_r.at[0], dev(to, z + 1, x)).start()

    def edges_sent(ref):
        @pl.when(k > 0)
        def _():
            arrived(ref.at[:, pl.ds(0, 16)], hl_s.at[0])

        @pl.when(k < WIN - 1)
        def _():
            arrived(ref.at[:, pl.ds(CELLS - 16, 16)], hl_s.at[1])

    @pl.when(k == 0)
    def _():
        halo[0] = jnp.zeros((FR, 16, C), BF16)

    @pl.when(k == WIN - 1)
    def _():
        halo[1] = jnp.zeros((FR, 16, C), BF16)

    def post(src, dst, ssem, rsem, to):
        @pl.when(to != z)
        def _():
            remote(src, dst, ssem, rsem, dev(seg, to, x)).start()

        @pl.when(to == z)
        def _():
            pltpu.make_async_copy(src, dst, rsem).start()

    def posted(src, ssem, to):
        @pl.when(to != z)
        def _():
            arrived(src, ssem)

    low, high = clips.at[:, :, pl.ds(0, 16)], clips.at[:, :, pl.ds(48, 16)]
    goes_up = jnp.logical_and(k == 0, m > 0)
    goes_down = jnp.logical_and(k == WIN - 1, m < WIN - 1)

    @pl.when(first)
    def _():
        regroup(clips, xin, cg_s, cg_r)
        for i in range(MB):
            @pl.when(goes_up)
            def _():
                post(low.at[i], halo.at[1], sc_s.at[16 + i], hl_r.at[1], i * WIN + m - 1)

            @pl.when(goes_down)
            def _():
                post(high.at[i], halo.at[0], sc_s.at[16 + i], hl_r.at[0], i * WIN + m + 1)

        for i in range(MB):
            here = lengths[i, 0]
            masks = [jnp.where(f < here, 1.0, 0.0).astype(F32) for f in range(FR)]
            st_clip[i, 0], st_clip[i, 1] = stats_of(clips.at[i], 8, masks, (here * 64).astype(F32))
            for kk in range(WIN):
                post(st_clip.at[i], st_in.at[z], sc_s.at[i * WIN + kk], sc_r.at[z], i * WIN + kk)

        regroup_recv(xin, cg_r)
        for j in range(ZS):
            arrived(st_in.at[j], sc_r.at[j])
        combine([(st_in[j, 0], st_in[j, 1]) for j in range(ZS)], (length * 64).astype(F32))

    @pl.when(seg > 1)
    def _():
        regroup(cot, cotz, ct_s, ct_r)

    @pl.when(seg > 0)
    def _():
        for h in range(2):
            arrived(xin.at[:, pl.ds(h * 128, 128)], rl_r.at[h])
        for kk in range(WIN):
            arrived(st_in.at[kk], st_r.at[kk])
        combine([(st_in[kk, 0], st_in[kk, 1]) for kk in range(WIN)], n_dev)

    @pl.when(k > 0)
    def _():
        arrived(halo.at[0], hl_r.at[0])

    @pl.when(k < WIN - 1)
    def _():
        arrived(halo.at[1], hl_r.at[1])

    mean = norm[0]
    scale = norm[1] * gain[...]
    offset = jnp.broadcast_to(shift[...], (8, C))
    col = lax.broadcasted_iota(jnp.int32, (1, 8, C), 1)

    def act(v):
        v = (v - mean[None]) * scale[None] + offset[None]
        return v / (1.0 + jnp.exp(-v))

    def put(row, n, per_frame):
        for fp in range(2):
            pair = [per_frame[2 * fp], per_frame[2 * fp + 1]]
            for d in range(3):
                if d == 0:
                    out = [jnp.where(col == 0, 0.0, pltpu.roll(h.reshape(n * 8, C), 1, 0).reshape(n, 8, C)) for h in pair]
                elif d == 2:
                    out = [jnp.where(col == 7, 0.0, pltpu.roll(h.reshape(n * 8, C), n * 8 - 1, 0).reshape(n, 8, C)) for h in pair]
                else:
                    out = pair
                hs[d, pl.ds(row, n), fp] = jnp.concatenate(out, axis=1).astype(BF16)

    top_here, bottom_here = k > 0, k < WIN - 1
    put(0, 1, [jnp.where(top_here, act(halo[0, f, 8:16].astype(F32).reshape(1, 8, C)), 0.0) for f in range(FR)])
    put(ROWS + 1, 1, [jnp.where(bottom_here, act(halo[1, f, 0:8].astype(F32).reshape(1, 8, C)), 0.0) for f in range(FR)])

    def norm_step(j, c):
        put(8 * j + 1, 8, [
            act(xin[f, pl.ds(pl.multiple_of(j * 64, 64), 64)].astype(F32).reshape(8, 8, C)) for f in range(FR)])
        return c

    lax.fori_loop(0, ROWS // 8, norm_step, 0)

    for cp in w_copies:
        cp.wait()

    factor = 1.0 / math.sqrt(MB * XS * FR * 128 * 8)

    def gradient():
        regroup_recv(cotz, ct_r)

        def rhs_step(j, c):
            cut = pl.ds(pl.multiple_of(j * 64, 64), 64)
            cs = [cotz[f, cut].astype(F32).reshape(8, 8, C) * mask[f] for f in range(FR)]
            zero = jnp.zeros((8, 8, C), F32)
            two = cs[0] + cs[1]
            cols = [
                [[two + cs[2], cs[3]], [zero, zero]],
                [[two, cs[2]], [cs[3], zero]],
                [[cs[0], cs[1]], [cs[2], cs[3]]],
            ]
            for a in range(3):
                for fp in range(2):
                    rhs[pl.ds(8 * j, 8), fp, :, a * C:(a + 1) * C] = jnp.concatenate(cols[a][fp], axis=1).astype(BF16)
            return c

        lax.fori_loop(0, ROWS // 8, rhs_step, 0)
        for b in range(CH):
            lhs = jnp.concatenate([hs[d, b:b + ROWS].reshape(ROWS * 32, C) for d in range(3)], axis=1)
            acc = lax.dot_general(
                lhs, rhs[...].reshape(ROWS * 32, 3 * C), (((0,), (0,)), ((), ())), preferred_element_type=F32)
            for a in range(3):
                block = (acc[:, a * C:(a + 1) * C] * factor).astype(BF16)
                for q in range(XS):
                    part[b, q, 3 * a:3 * a + 3] = block[96 * q:96 * q + 96].reshape(3, PR, C)
            for o in (2, 1, 3):
                to = lax.rem(x + o, XS)
                remote(part.at[b, to], xr.at[b, o - 1], xs_s.at[b, o - 1], xs_r.at[b, o - 1],
                       dev(seg, z, to)).start()

    @pl.when(last)
    def _():
        gradient()

    bias_row = bias[...].reshape(1, 1, C)
    half = ROWS // 2
    for h in range(2):
        def taps(fp):
            return jnp.concatenate(
                [hs[d, pl.ds(h * half + b, half), fp].reshape(half * 16, C) for b in range(3) for d in range(3)], axis=1)

        p01 = jnp.dot(taps(0), wcat[...], preferred_element_type=F32).reshape(half, 2, 8, 3 * C)
        p23 = jnp.dot(taps(1), wcat[:, C:], preferred_element_type=F32).reshape(half, 2, 8, 2 * C)
        a0, a1, a2 = slice(0, C), slice(C, 2 * C), slice(2 * C, 3 * C)
        early = p01[:, 0, :, a0] + p01[:, 0, :, a1]
        outs = [
            early + p01[:, 0, :, a2],
            early + p01[:, 1, :, a2],
            p01[:, 0, :, a0] + p01[:, 1, :, a1] + p23[:, 0, :, a1],
            p01[:, 1, :, a0] + p23[:, 0, :, a0] + p23[:, 1, :, a1],
        ]
        for f in range(FR):
            v = xin[f, h * 128:(h + 1) * 128].astype(F32).reshape(half, 8, C)
            out = (v + outs[f] + bias_row) * mask[f]
            xout[f, h * 128:(h + 1) * 128] = out.reshape(128, C).astype(BF16)

        @pl.when(jnp.logical_not(last))
        def _():
            part_h = (slice(None), pl.ds(h * 128, 128))
            remote(xout.at[part_h], xin.at[part_h], rl_s.at[h], rl_r.at[h], dev(nxt, z, x)).start()

    @pl.when(jnp.logical_not(last))
    def _():
        send_edges(xout, nxt)
        st_out[0], st_out[1] = stats_of(xout, ROWS, mask, n_dev)
        for kk in range(WIN):
            remote(st_out, st_in.at[k], st_s.at[kk], st_r.at[k], dev(nxt, m * WIN + kk, x)).start()

    @pl.when(jnp.logical_and(seg % 2 == 1, jnp.logical_not(last)))
    def _():
        pl.semaphore_signal(go, inc=1, device_id=dev(seg - 1, z, x), device_id_type=MESH)

    @pl.when(jnp.logical_and(seg % 2 == 0, seg < SEGS - 2))
    def _():
        pl.semaphore_wait(go, 1)

    @pl.when(seg <= 1)
    def _():
        regroup(cot, cotz, ct_s, ct_r)

    for j in range(WIN):
        to = k * WIN + j
        src = xout.at[:, pl.ds(j * 64, 64)]

        @pl.when(to != z)
        def _():
            remote(src, stash.at[m], ss_s.at[j], ss_r.at[m], dev(seg, to, x)).start()

        @pl.when(to == z)
        def _():
            pltpu.make_async_copy(src, stash.at[m], ss_r.at[m]).start()

    @pl.when(jnp.logical_not(last))
    def _():
        gradient()

    order = (8, 7, 9, 6, 10, 5, 11, 4, 12, 3, 13, 2, 14, 1, 15)

    def piece(c, zz):
        return lax.rem(zz + 2 * ZS - PC * c, ZS)

    for c in range(CH):
        for o in (1, 3, 2):
            arrived(xr.at[c, o - 1], xs_r.at[c, o - 1])
        for p in range(PC):
            v = part[c, x, p].astype(F32)
            for o in range(3):
                v = v + xr[c, o, p].astype(F32)
            zs[c, p] = v.astype(BF16)
        for o in order:
            to = lax.rem(z + o, ZS)
            p_to = piece(c, to)

            @pl.when(p_to < PC)
            def _():
                remote(zs.at[c, p_to], zr.at[c, o - 1], zs_s.at[c, o - 1], zs_r.at[c, o - 1], dev(seg, to, x)).start()

    for c in range(CH):
        mine = piece(c, z)

        @pl.when(mine < PC)
        def _():
            v = zs[c, mine].astype(F32)
            for o in order[::-1]:
                arrived(zr.at[c, o - 1], zs_r.at[c, o - 1])
                v = v + zr[c, o - 1].astype(F32)
            kept = grad.at[mine // 3, c, 3 * x + mine % 3]
            kept[...] = v.astype(BF16)
            for o in order:
                remote(kept, kept, ag_s.at[c, o - 1], ag_r.at[c, o - 1], dev(seg, lax.rem(z + o, ZS), x)).start()

    for c in range(CH):
        for o in order[::-1]:
            p_src = piece(c, lax.rem(z + ZS - o, ZS))

            @pl.when(p_src < PC)
            def _():
                arrived(zr.at[c, o - 1], ag_r.at[c, o - 1])

        quarter = grad.at[:, c, pl.ds(3 * x, 3)]
        for o in (2, 1, 3):
            remote(quarter, quarter, xg_s.at[c, o - 1], xg_r.at[c, o - 1], dev(seg, z, lax.rem(x + o, XS))).start()

    for j in range(MB):
        arrived(stash.at[j], ss_r.at[j])
    for j in range(WIN):
        @pl.when(k * WIN + j != z)
        def _():
            arrived(xout.at[:, pl.ds(j * 64, 64)], ss_s.at[j])

    regroup_sent(cot, ct_s)

    @pl.when(jnp.logical_not(last))
    def _():
        for h in range(2):
            arrived(xout.at[:, pl.ds(h * 128, 128)], rl_s.at[h])
        for kk in range(WIN):
            arrived(st_out, st_s.at[kk])
        edges_sent(xout)

    @pl.when(first)
    def _():
        regroup_sent(clips, cg_s)
        for i in range(MB):
            for kk in range(WIN):
                posted(st_clip.at[i], sc_s.at[i * WIN + kk], i * WIN + kk)

            @pl.when(goes_up)
            def _():
                posted(low.at[i], sc_s.at[16 + i], i * WIN + m - 1)

            @pl.when(goes_down)
            def _():
                posted(high.at[i], sc_s.at[16 + i], i * WIN + m + 1)

    for c in range(CH):
        for o in range(1, XS):
            arrived(xr.at[c, o - 1], xs_s.at[c, o - 1])
        for o in range(1, ZS):
            @pl.when(piece(c, lax.rem(z + o, ZS)) < PC)
            def _():
                arrived(zr.at[c, o - 1], zs_s.at[c, o - 1])

        @pl.when(piece(c, z) < PC)
        def _():
            for o in range(1, ZS):
                arrived(zr.at[c, o - 1], ag_s.at[c, o - 1])

    for c in range(CH):
        for o in range(1, XS):
            arrived(grad.at[:, c, pl.ds(3 * lax.rem(x + XS - o, XS), 3)], xg_r.at[c, o - 1])
            arrived(xr.at[c, o - 1], xg_s.at[c, o - 1])


def per_device(clips, lengths, conv_weight, norm_gain, norm_shift, conv_bias, cotangent):
    vmem, anyspace = pltpu.VMEM, pl.ANY
    dma = pltpu.SemaphoreType.DMA
    stash, grad = pl.pallas_call(
        kernel,
        out_shape=(
            jax.ShapeDtypeStruct((MB, FR, 64, C), BF16),
            jax.ShapeDtypeStruct((3, CH, 12, PR, C), BF16),
        ),
        in_specs=[pl.BlockSpec(memory_space=anyspace)] * 7,
        out_specs=(pl.BlockSpec(memory_space=vmem), pl.BlockSpec(memory_space=vmem)),
        scratch_shapes=[
            vmem((MB, FR, 64, C), BF16),
            pltpu.SMEM((MB, 1), jnp.int32),
            vmem((1, C), F32), vmem((1, C), F32), vmem((1, C), F32),
            vmem((FR, CELLS, C), BF16),
            vmem((FR, CELLS, C), BF16),
            vmem((2, FR, 16, C), BF16),
            vmem((9 * C, 3 * C), BF16),
            vmem((3, ROWS + 2, 2, 16, C), BF16),
            vmem((FR, CELLS, C), BF16),
            vmem((ROWS, 2, 16, 3 * C), BF16),
            vmem((CH, XS, PC, PR, C), BF16),
            vmem((CH, XS - 1, PC, PR, C), BF16),
            vmem((CH, PC, PR, C), BF16),
            vmem((CH, ZS - 1, PR, C), BF16),
            vmem((2, 8, C), F32),
            vmem((ZS, 2, 8, C), F32),
            vmem((MB, 2, 8, C), F32),
            vmem((2, 8, C), F32),
            pltpu.SemaphoreType.REGULAR,
            dma((5,)),
            dma((3,)),
            dma((4,)), dma((4,)), dma((4,)), dma((4,)), dma((4,)), dma((4,)),
            dma((2,)), dma((2,)), dma((2,)), dma((2,)), dma((4,)), dma((4,)),
            dma((20,)), dma((16,)),
            dma((3, 3)), dma((3, 3)), dma((3, 15)), dma((3, 15)), dma((3, 15)), dma((3, 15)), dma((3, 3)), dma((3, 3)),
        ],
        compiler_params=pltpu.CompilerParams(
            collective_id=0, has_side_effects=True, vmem_limit_bytes=63 * 2**20),
        cost_estimate=pl.CostEstimate(flops=2 * 10**9, bytes_accessed=4 * 10**6, transcendentals=10**6),
    )(
        clips.reshape(MB, FR, 64, C), lengths, conv_weight[0], norm_gain, norm_shift, conv_bias,
        cotangent.reshape(MB, FR, 64, C))
    grads = grad.reshape(27 * C, C).astype(F32)
    return stash.reshape(1, MB, 1, FR, 8, 8, C), grads[None]


def solution(mesh):
    in_specs = (
        P(None, "dp", None, "rows", None, None),
        P(None, "dp"),
        P("segment", None, None),
        P("segment", None),
        P("segment", None),
        P("segment", None),
        P("segment", None, "dp", None, "rows", None, None),
    )
    out_specs = (P("segment", None, "dp", None, "rows", None, None), P("segment", None, None))
    return jax.shard_map(per_device, mesh=mesh, in_specs=in_specs, out_specs=out_specs, check_vma=False)
```

```python
import math

import jax
import jax.numpy as jnp
from jax import lax
from jax.experimental import pallas as pl
from jax.experimental.pallas import tpu as pltpu
from jax.sharding import PartitionSpec as P

MESH = pl.DeviceIdType.MESH
EPS = 1e-06
SEGS, ZS, XS, MB, FR, C = 8, 16, 4, 4, 4, 128
WIN = 4
ROWS = 32
CELLS = ROWS * 8
CH, PC, PR = 3, 9, 32
F32, BF16 = jnp.float32, jnp.bfloat16


def group_sum(v):
    lane = lax.broadcasted_iota(jnp.int32, v.shape, 1)
    v = v + jnp.where(lane % 2 == 0, pltpu.roll(v, 127, 1), pltpu.roll(v, 1, 1))
    return v + jnp.where(lane % 4 < 2, pltpu.roll(v, 126, 1), pltpu.roll(v, 2, 1))


def kernel(clips_any, lengths_any, w, gain_any, shift_any, bias_any, cot, stash, grad,
           clips, lengths, gain, shift, bias,
           xin, xout, halo, wcat, hs, cotz, rhs, part, xr, zs, zr, st_out, st_in, st_clip, norm, go,
           in_sem, w_sem, cg_s, cg_r, ct_s, ct_r, ss_s, ss_r, rl_s, rl_r, hl_s, hl_r, st_s, st_r,
           sc_s, sc_r,
           xs_s, xs_r, zs_s, zs_r, ag_s, ag_r, xg_s, xg_r):
    seg = lax.axis_index("segment")
    z = lax.axis_index("rows")
    x = lax.axis_index("dp")
    m = z // WIN
    k = z % WIN
    nxt = lax.rem(seg + 1, SEGS)
    prv = lax.rem(seg + SEGS - 1, SEGS)
    first = seg == 0
    last = seg == SEGS - 1

    def dev(s, zz, xx):
        return {"segment": s, "rows": zz, "dp": xx}

    def remote(src, dst, ssem, rsem, target):
        return pltpu.make_async_remote_copy(
            src_ref=src, dst_ref=dst, send_sem=ssem, recv_sem=rsem, device_id=target, device_id_type=MESH)

    def arrived(ref, sem):
        pltpu.make_async_copy(ref, ref, sem).wait()

    in_copies = [
        pltpu.make_async_copy(src, dst, in_sem.at[i])
        for i, (src, dst) in enumerate([
            (clips_any, clips), (lengths_any, lengths), (gain_any, gain), (shift_any, shift), (bias_any, bias)])
    ]
    for cp in in_copies:
        cp.start()

    w_copies = [
        pltpu.make_async_copy(w.at[pl.ds(a * 9 * C, 9 * C)], wcat.at[:, pl.ds(a * C, C)], w_sem.at[a])
        for a in range(3)
    ]
    for cp in w_copies:
        cp.start()

    bar = pltpu.get_barrier_semaphore()

    def greet(target):
        pl.semaphore_signal(bar, inc=1, device_id=target, device_id_type=MESH)

    for o in range(1, ZS):
        greet(dev(seg, lax.rem(z + o, ZS), x))
    for o in range(1, XS):
        greet(dev(seg, z, lax.rem(x + o, XS)))
    for kk in range(WIN):
        greet(dev(nxt, m * WIN + kk, x))
        greet(dev(prv, m * WIN + kk, x))
    for cp in in_copies:
        cp.wait()
    pl.semaphore_wait(bar, ZS - 1 + XS - 1 + 2 * WIN)

    def regroup(src, dst, ssem, rsem):
        for i in range(MB):
            to = i * WIN + m
            here = dst.at[:, pl.ds(pl.multiple_of(k * 64, 64), 64)]

            @pl.when(to != z)
            def _():
                remote(src.at[i], here, ssem.at[i], rsem.at[k], dev(seg, to, x)).start()

            @pl.when(to == z)
            def _():
                pltpu.make_async_copy(src.at[i], here, rsem.at[k]).start()

    def regroup_recv(dst, rsem):
        for j in range(WIN):
            arrived(dst.at[:, pl.ds(j * 64, 64)], rsem.at[j])

    def regroup_sent(src, ssem):
        for i in range(MB):
            @pl.when(i * WIN + m != z)
            def _():
                arrived(src.at[i], ssem.at[i])

    length = lengths[m]
    mask = [jnp.where(f < length, 1.0, 0.0).astype(F32) for f in range(FR)]
    n_dev = (length * CELLS).astype(F32)

    def stats_of(ref, rows, masks, n):
        def over(fn):
            total = jnp.zeros((8, C), F32)
            for f in range(FR):
                total = total + jnp.sum(fn(ref[f].astype(F32).reshape(rows, 8, C)), axis=0) * masks[f]
            return jnp.broadcast_to(jnp.sum(total, axis=0, keepdims=True), (8, C))

        sums = over(lambda v: v)
        mean = (sums / n)[None]
        return sums, over(lambda v: (v - mean) * (v - mean))

    def combine(parts, n):
        count = n * (4.0 * len(parts))
        total = parts[0][0]
        for sums, _ in parts[1:]:
            total = total + sums
        mean = group_sum(total) / count
        spread = jnp.zeros((8, C), F32)
        for sums, squares in parts:
            off = sums / n - mean
            spread = spread + squares + n * (off * off)
        norm[0] = mean
        norm[1] = lax.rsqrt(group_sum(spread) / count + EPS)

    def send_edges(ref, to):
        @pl.when(k > 0)
        def _():
            remote(ref.at[:, pl.ds(0, 16)], halo.at[1], hl_s.at[0], hl_r.at[1], dev(to, z - 1, x)).start()

        @pl.when(k < WIN - 1)
        def _():
            remote(ref.at[:, pl.ds(CELLS - 16, 16)], halo.at[0], hl_s.at[1], hl_r.at[0], dev(to, z + 1, x)).start()

    def edges_sent(ref):
        @pl.when(k > 0)
        def _():
            arrived(ref.at[:, pl.ds(0, 16)], hl_s.at[0])

        @pl.when(k < WIN - 1)
        def _():
            arrived(ref.at[:, pl.ds(CELLS - 16, 16)], hl_s.at[1])

    @pl.when(k == 0)
    def _():
        halo[0] = jnp.zeros((FR, 16, C), BF16)

    @pl.when(k == WIN - 1)
    def _():
        halo[1] = jnp.zeros((FR, 16, C), BF16)

    def post(src, dst, ssem, rsem, to):
        @pl.when(to != z)
        def _():
            remote(src, dst, ssem, rsem, dev(seg, to, x)).start()

        @pl.when(to == z)
        def _():
            pltpu.make_async_copy(src, dst, rsem).start()

    def posted(src, ssem, to):
        @pl.when(to != z)
        def _():
            arrived(src, ssem)

    low, high = clips.at[:, :, pl.ds(0, 16)], clips.at[:, :, pl.ds(48, 16)]
    goes_up = jnp.logical_and(k == 0, m > 0)
    goes_down = jnp.logical_and(k == WIN - 1, m < WIN - 1)

    @pl.when(first)
    def _():
        regroup(clips, xin, cg_s, cg_r)
        for i in range(MB):
            @pl.when(goes_up)
            def _():
                post(low.at[i], halo.at[1], sc_s.at[16 + i], hl_r.at[1], i * WIN + m - 1)

            @pl.when(goes_down)
            def _():
                post(high.at[i], halo.at[0], sc_s.at[16 + i], hl_r.at[0], i * WIN + m + 1)

        for i in range(MB):
            here = lengths[i]
            masks = [jnp.where(f < here, 1.0, 0.0).astype(F32) for f in range(FR)]
            st_clip[i, 0], st_clip[i, 1] = stats_of(clips.at[i], 8, masks, (here * 64).astype(F32))
            for kk in range(WIN):
                post(st_clip.at[i], st_in.at[z], sc_s.at[i * WIN + kk], sc_r.at[z], i * WIN + kk)

        regroup_recv(xin, cg_r)
        for j in range(ZS):
            arrived(st_in.at[j], sc_r.at[j])
        combine([(st_in[j, 0], st_in[j, 1]) for j in range(ZS)], (length * 64).astype(F32))

    @pl.when(seg > 1)
    def _():
        regroup(cot, cotz, ct_s, ct_r)

    @pl.when(seg > 0)
    def _():
        for h in range(2):
            arrived(xin.at[:, pl.ds(h * 128, 128)], rl_r.at[h])
        for kk in range(WIN):
            arrived(st_in.at[kk], st_r.at[kk])
        combine([(st_in[kk, 0], st_in[kk, 1]) for kk in range(WIN)], n_dev)

    @pl.when(k > 0)
    def _():
        arrived(halo.at[0], hl_r.at[0])

    @pl.when(k < WIN - 1)
    def _():
        arrived(halo.at[1], hl_r.at[1])

    mean = norm[0]
    scale = norm[1] * gain[...]
    offset = jnp.broadcast_to(shift[...], (8, C))
    col = lax.broadcasted_iota(jnp.int32, (1, 8, C), 1)

    def act(v):
        v = (v - mean[None]) * scale[None] + offset[None]
        return v / (1.0 + jnp.exp(-v))

    def put(row, n, per_frame):
        for fp in range(2):
            pair = [per_frame[2 * fp], per_frame[2 * fp + 1]]
            for d in range(3):
                if d == 0:
                    out = [jnp.where(col == 0, 0.0, pltpu.roll(h.reshape(n * 8, C), 1, 0).reshape(n, 8, C)) for h in pair]
                elif d == 2:
                    out = [jnp.where(col == 7, 0.0, pltpu.roll(h.reshape(n * 8, C), n * 8 - 1, 0).reshape(n, 8, C)) for h in pair]
                else:
                    out = pair
                hs[d, pl.ds(row, n), fp] = jnp.concatenate(out, axis=1).astype(BF16)

    top_here, bottom_here = k > 0, k < WIN - 1
    put(0, 1, [jnp.where(top_here, act(halo[0, f, 8:16].astype(F32).reshape(1, 8, C)), 0.0) for f in range(FR)])
    put(ROWS + 1, 1, [jnp.where(bottom_here, act(halo[1, f, 0:8].astype(F32).reshape(1, 8, C)), 0.0) for f in range(FR)])

    def norm_step(j, c):
        put(8 * j + 1, 8, [
            act(xin[f, pl.ds(pl.multiple_of(j * 64, 64), 64)].astype(F32).reshape(8, 8, C)) for f in range(FR)])
        return c

    lax.fori_loop(0, ROWS // 8, norm_step, 0)

    for cp in w_copies:
        cp.wait()

    factor = 1.0 / math.sqrt(MB * XS * FR * 128 * 8)

    def gradient():
        regroup_recv(cotz, ct_r)

        def rhs_step(j, c):
            cut = pl.ds(pl.multiple_of(j * 64, 64), 64)
            cs = [cotz[f, cut].astype(F32).reshape(8, 8, C) * mask[f] for f in range(FR)]
            zero = jnp.zeros((8, 8, C), F32)
            two = cs[0] + cs[1]
            cols = [
                [[two + cs[2], cs[3]], [zero, zero]],
                [[two, cs[2]], [cs[3], zero]],
                [[cs[0], cs[1]], [cs[2], cs[3]]],
            ]
            for a in range(3):
                for fp in range(2):
                    rhs[pl.ds(8 * j, 8), fp, :, a * C:(a + 1) * C] = jnp.concatenate(cols[a][fp], axis=1).astype(BF16)
            return c

        lax.fori_loop(0, ROWS // 8, rhs_step, 0)
        for b in range(CH):
            lhs = jnp.concatenate([hs[d, b:b + ROWS].reshape(ROWS * 32, C) for d in range(3)], axis=1)
            acc = lax.dot_general(
                lhs, rhs[...].reshape(ROWS * 32, 3 * C), (((0,), (0,)), ((), ())), preferred_element_type=F32)
            for a in range(3):
                block = (acc[:, a * C:(a + 1) * C] * factor).astype(BF16)
                for q in range(XS):
                    part[b, q, 3 * a:3 * a + 3] = block[96 * q:96 * q + 96].reshape(3, PR, C)
            for o in (2, 1, 3):
                to = lax.rem(x + o, XS)
                remote(part.at[b, to], xr.at[b, o - 1], xs_s.at[b, o - 1], xs_r.at[b, o - 1],
                       dev(seg, z, to)).start()

    @pl.when(last)
    def _():
        gradient()

    bias_row = bias[...].reshape(1, 1, C)
    half = ROWS // 2
    for h in range(2):
        def taps(fp):
            return jnp.concatenate(
                [hs[d, pl.ds(h * half + b, half), fp].reshape(half * 16, C) for b in range(3) for d in range(3)], axis=1)

        p01 = jnp.dot(taps(0), wcat[...], preferred_element_type=F32).reshape(half, 2, 8, 3 * C)
        p23 = jnp.dot(taps(1), wcat[:, C:], preferred_element_type=F32).reshape(half, 2, 8, 2 * C)
        a0, a1, a2 = slice(0, C), slice(C, 2 * C), slice(2 * C, 3 * C)
        early = p01[:, 0, :, a0] + p01[:, 0, :, a1]
        outs = [
            early + p01[:, 0, :, a2],
            early + p01[:, 1, :, a2],
            p01[:, 0, :, a0] + p01[:, 1, :, a1] + p23[:, 0, :, a1],
            p01[:, 1, :, a0] + p23[:, 0, :, a0] + p23[:, 1, :, a1],
        ]
        for f in range(FR):
            v = xin[f, h * 128:(h + 1) * 128].astype(F32).reshape(half, 8, C)
            out = (v + outs[f] + bias_row) * mask[f]
            xout[f, h * 128:(h + 1) * 128] = out.reshape(128, C).astype(BF16)

        @pl.when(jnp.logical_not(last))
        def _():
            part_h = (slice(None), pl.ds(h * 128, 128))
            remote(xout.at[part_h], xin.at[part_h], rl_s.at[h], rl_r.at[h], dev(nxt, z, x)).start()

    @pl.when(jnp.logical_not(last))
    def _():
        send_edges(xout, nxt)
        st_out[0], st_out[1] = stats_of(xout, ROWS, mask, n_dev)
        for kk in range(WIN):
            remote(st_out, st_in.at[k], st_s.at[kk], st_r.at[k], dev(nxt, m * WIN + kk, x)).start()

    def send_stash():
        for j in range(WIN):
            to = k * WIN + j
            src = xout.at[:, pl.ds(j * 64, 64)]

            @pl.when(to != z)
            def _():
                remote(src, stash.at[m], ss_s.at[j], ss_r.at[m], dev(seg, to, x)).start()

            @pl.when(to == z)
            def _():
                pltpu.make_async_copy(src, stash.at[m], ss_r.at[m]).start()

    @pl.when(jnp.logical_and(seg % 2 == 1, jnp.logical_not(last)))
    def _():
        pl.semaphore_signal(go, inc=1, device_id=dev(seg - 1, z, x), device_id_type=MESH)

    @pl.when(first)
    def _():
        pl.semaphore_wait(go, 1)

    @pl.when(seg <= 1)
    def _():
        regroup(cot, cotz, ct_s, ct_r)

    @pl.when(seg == SEGS - 2)
    def _():
        send_stash()

    @pl.when(jnp.logical_not(last))
    def _():
        gradient()

    order = (8, 7, 9, 6, 10, 5, 11, 4, 12, 3, 13, 2, 14, 1, 15)

    def piece(c, zz):
        return lax.rem(zz + 2 * ZS - PC * c, ZS)

    @pl.when(jnp.logical_and(seg % 2 == 0, jnp.logical_and(seg > 0, seg < SEGS - 2)))
    def _():
        pl.semaphore_wait(go, 1)

    for c in range(CH):
        for o in (1, 3, 2):
            arrived(xr.at[c, o - 1], xs_r.at[c, o - 1])
        for p in range(PC):
            v = part[c, x, p].astype(F32)
            for o in range(3):
                v = v + xr[c, o, p].astype(F32)
            zs[c, p] = v.astype(BF16)
        for o in order:
            to = lax.rem(z + o, ZS)
            p_to = piece(c, to)

            @pl.when(p_to < PC)
            def _():
                remote(zs.at[c, p_to], zr.at[c, o - 1], zs_s.at[c, o - 1], zs_r.at[c, o - 1], dev(seg, to, x)).start()

    @pl.when(seg != SEGS - 2)
    def _():
        send_stash()

    for c in range(CH):
        mine = piece(c, z)

        @pl.when(mine < PC)
        def _():
            v = zs[c, mine].astype(F32)
            for o in order[::-1]:
                arrived(zr.at[c, o - 1], zs_r.at[c, o - 1])
                v = v + zr[c, o - 1].astype(F32)
            kept = grad.at[mine // 3, c, 3 * x + mine % 3]
            kept[...] = v.astype(BF16)
            for o in order:
                remote(kept, kept, ag_s.at[c, o - 1], ag_r.at[c, o - 1], dev(seg, lax.rem(z + o, ZS), x)).start()

    for c in range(CH):
        for o in order[::-1]:
            p_src = piece(c, lax.rem(z + ZS - o, ZS))

            @pl.when(p_src < PC)
            def _():
                arrived(zr.at[c, o - 1], ag_r.at[c, o - 1])

        quarter = grad.at[:, c, pl.ds(3 * x, 3)]
        for o in (2, 1, 3):
            remote(quarter, quarter, xg_s.at[c, o - 1], xg_r.at[c, o - 1], dev(seg, z, lax.rem(x + o, XS))).start()

    for j in range(MB):
        arrived(stash.at[j], ss_r.at[j])
    for j in range(WIN):
        @pl.when(k * WIN + j != z)
        def _():
            arrived(xout.at[:, pl.ds(j * 64, 64)], ss_s.at[j])

    regroup_sent(cot, ct_s)

    @pl.when(jnp.logical_not(last))
    def _():
        for h in range(2):
            arrived(xout.at[:, pl.ds(h * 128, 128)], rl_s.at[h])
        for kk in range(WIN):
            arrived(st_out, st_s.at[kk])
        edges_sent(xout)

    @pl.when(first)
    def _():
        regroup_sent(clips, cg_s)
        for i in range(MB):
            for kk in range(WIN):
                posted(st_clip.at[i], sc_s.at[i * WIN + kk], i * WIN + kk)

            @pl.when(goes_up)
            def _():
                posted(low.at[i], sc_s.at[16 + i], i * WIN + m - 1)

            @pl.when(goes_down)
            def _():
                posted(high.at[i], sc_s.at[16 + i], i * WIN + m + 1)

    for c in range(CH):
        for o in range(1, XS):
            arrived(xr.at[c, o - 1], xs_s.at[c, o - 1])
        for o in range(1, ZS):
            @pl.when(piece(c, lax.rem(z + o, ZS)) < PC)
            def _():
                arrived(zr.at[c, o - 1], zs_s.at[c, o - 1])

        @pl.when(piece(c, z) < PC)
        def _():
            for o in range(1, ZS):
                arrived(zr.at[c, o - 1], ag_s.at[c, o - 1])

    for c in range(CH):
        for o in range(1, XS):
            arrived(grad.at[:, c, pl.ds(3 * lax.rem(x + XS - o, XS), 3)], xg_r.at[c, o - 1])
            arrived(xr.at[c, o - 1], xg_s.at[c, o - 1])


def per_device(clips, lengths, conv_weight, norm_gain, norm_shift, conv_bias, cotangent):
    vmem, anyspace = pltpu.VMEM, pl.ANY
    dma = pltpu.SemaphoreType.DMA
    stash, grad = pl.pallas_call(
        kernel,
        out_shape=(
            jax.ShapeDtypeStruct((MB, FR, 64, C), BF16),
            jax.ShapeDtypeStruct((3, CH, 12, PR, C), BF16),
        ),
        in_specs=[pl.BlockSpec(memory_space=anyspace)] * 7,
        out_specs=(pl.BlockSpec(memory_space=vmem), pl.BlockSpec(memory_space=vmem)),
        scratch_shapes=[
            vmem((MB, FR, 64, C), BF16),
            pltpu.SMEM((MB,), jnp.int32),
            vmem((1, C), F32), vmem((1, C), F32), vmem((1, C), F32),
            vmem((FR, CELLS, C), BF16),
            vmem((FR, CELLS, C), BF16),
            vmem((2, FR, 16, C), BF16),
            vmem((9 * C, 3 * C), BF16),
            vmem((3, ROWS + 2, 2, 16, C), BF16),
            vmem((FR, CELLS, C), BF16),
            vmem((ROWS, 2, 16, 3 * C), BF16),
            vmem((CH, XS, PC, PR, C), BF16),
            vmem((CH, XS - 1, PC, PR, C), BF16),
            vmem((CH, PC, PR, C), BF16),
            vmem((CH, ZS - 1, PR, C), BF16),
            vmem((2, 8, C), F32),
            vmem((ZS, 2, 8, C), F32),
            vmem((MB, 2, 8, C), F32),
            vmem((2, 8, C), F32),
            pltpu.SemaphoreType.REGULAR,
            dma((5,)),
            dma((3,)),
            dma((4,)), dma((4,)), dma((4,)), dma((4,)), dma((4,)), dma((4,)),
            dma((2,)), dma((2,)), dma((2,)), dma((2,)), dma((4,)), dma((4,)),
            dma((20,)), dma((16,)),
            dma((3, 3)), dma((3, 3)), dma((3, 15)), dma((3, 15)), dma((3, 15)), dma((3, 15)), dma((3, 3)), dma((3, 3)),
        ],
        compiler_params=pltpu.CompilerParams(
            collective_id=0, has_side_effects=True, vmem_limit_bytes=63 * 2**20),
        cost_estimate=pl.CostEstimate(flops=2 * 10**9, bytes_accessed=4 * 10**6, transcendentals=10**6),
    )(
        clips.reshape(MB, FR, 64, C), lengths.reshape(MB), conv_weight[0], norm_gain, norm_shift, conv_bias,
        cotangent.reshape(MB, FR, 64, C))
    grads = grad.reshape(27 * C, C).astype(F32)
    return stash.reshape(1, MB, 1, FR, 8, 8, C), grads[None]


def solution(mesh):
    in_specs = (
        P(None, "dp", None, "rows", None, None),
        P(None, "dp"),
        P("segment", None, None),
        P("segment", None),
        P("segment", None),
        P("segment", None),
        P("segment", None, "dp", None, "rows", None, None),
    )
    out_specs = (P("segment", None, "dp", None, "rows", None, None), P("segment", None, None))
    return jax.shard_map(per_device, mesh=mesh, in_specs=in_specs, out_specs=out_specs, check_vma=False)
```

```python
import math

import jax
import jax.numpy as jnp
from jax import lax
from jax.experimental import pallas as pl
from jax.experimental.pallas import tpu as pltpu
from jax.sharding import PartitionSpec as P

MESH = pl.DeviceIdType.MESH
EPS = 1e-06
SEGS, ZS, XS, MB, FR, C = 8, 16, 4, 4, 4, 128
WIN = 4
ROWS = 32
CELLS = ROWS * 8
CH, PC, PR = 3, 9, 32
F32, BF16 = jnp.float32, jnp.bfloat16


def group_sum(v):
    lane = lax.broadcasted_iota(jnp.int32, v.shape, 1)
    v = v + jnp.where(lane % 2 == 0, pltpu.roll(v, 127, 1), pltpu.roll(v, 1, 1))
    return v + jnp.where(lane % 4 < 2, pltpu.roll(v, 126, 1), pltpu.roll(v, 2, 1))


def kernel(clips_any, lengths_any, w, gain_any, shift_any, bias_any, cot, stash, grad,
           clips, lengths, gain, shift, bias,
           xin, xout, halo, wcat, hs, cotz, rhs, part, xr, zs, zr, st_out, st_in, st_clip, norm, go,
           in_sem, w_sem, cg_s, cg_r, ct_s, ct_r, ss_s, ss_r, rl_s, rl_r, hl_s, hl_r, st_s, st_r,
           sc_s, sc_r,
           xs_s, xs_r, zs_s, zs_r, ag_s, ag_r, xg_s, xg_r):
    seg = lax.axis_index("segment")
    z = lax.axis_index("rows")
    x = lax.axis_index("dp")
    m = z // WIN
    k = z % WIN
    nxt = lax.rem(seg + 1, SEGS)
    prv = lax.rem(seg + SEGS - 1, SEGS)
    first = seg == 0
    last = seg == SEGS - 1

    def dev(s, zz, xx):
        return {"segment": s, "rows": zz, "dp": xx}

    def remote(src, dst, ssem, rsem, target):
        return pltpu.make_async_remote_copy(
            src_ref=src, dst_ref=dst, send_sem=ssem, recv_sem=rsem, device_id=target, device_id_type=MESH)

    def arrived(ref, sem):
        pltpu.make_async_copy(ref, ref, sem).wait()

    in_copies = [
        pltpu.make_async_copy(src, dst, in_sem.at[i])
        for i, (src, dst) in enumerate([
            (clips_any, clips), (lengths_any, lengths), (gain_any, gain), (shift_any, shift), (bias_any, bias)])
    ]
    for cp in in_copies:
        cp.start()

    w_copies = [
        pltpu.make_async_copy(w.at[pl.ds(a * 9 * C, 9 * C)], wcat.at[:, pl.ds(a * C, C)], w_sem.at[a])
        for a in range(3)
    ]
    for cp in w_copies:
        cp.start()

    bar = pltpu.get_barrier_semaphore()

    def greet(target):
        pl.semaphore_signal(bar, inc=1, device_id=target, device_id_type=MESH)

    for o in range(1, ZS):
        greet(dev(seg, lax.rem(z + o, ZS), x))
    for o in range(1, XS):
        greet(dev(seg, z, lax.rem(x + o, XS)))
    for kk in range(WIN):
        greet(dev(nxt, m * WIN + kk, x))
        greet(dev(prv, m * WIN + kk, x))
    for cp in in_copies:
        cp.wait()
    pl.semaphore_wait(bar, ZS - 1 + XS - 1 + 2 * WIN)

    def regroup(src, dst, ssem, rsem):
        for i in range(MB):
            to = i * WIN + m
            here = dst.at[:, pl.ds(pl.multiple_of(k * 64, 64), 64)]

            @pl.when(to != z)
            def _():
                remote(src.at[i], here, ssem.at[i], rsem.at[k], dev(seg, to, x)).start()

            @pl.when(to == z)
            def _():
                pltpu.make_async_copy(src.at[i], here, rsem.at[k]).start()

    def regroup_recv(dst, rsem):
        for j in range(WIN):
            arrived(dst.at[:, pl.ds(j * 64, 64)], rsem.at[j])

    def regroup_sent(src, ssem):
        for i in range(MB):
            @pl.when(i * WIN + m != z)
            def _():
                arrived(src.at[i], ssem.at[i])

    length = lengths[m]
    mask = [jnp.where(f < length, 1.0, 0.0).astype(F32) for f in range(FR)]
    n_dev = (length * CELLS).astype(F32)

    def stats_of(ref, rows, masks, n):
        def over(fn):
            total = jnp.zeros((8, C), F32)
            for f in range(FR):
                total = total + jnp.sum(fn(ref[f].astype(F32).reshape(rows, 8, C)), axis=0) * masks[f]
            return jnp.broadcast_to(jnp.sum(total, axis=0, keepdims=True), (8, C))

        sums = over(lambda v: v)
        mean = (sums / n)[None]
        return sums, over(lambda v: (v - mean) * (v - mean))

    def combine(parts, n):
        count = n * (4.0 * len(parts))
        total = parts[0][0]
        for sums, _ in parts[1:]:
            total = total + sums
        mean = group_sum(total) / count
        spread = jnp.zeros((8, C), F32)
        for sums, squares in parts:
            off = sums / n - mean
            spread = spread + squares + n * (off * off)
        norm[0] = mean
        norm[1] = lax.rsqrt(group_sum(spread) / count + EPS)

    def send_edges(ref, to):
        @pl.when(k > 0)
        def _():
            remote(ref.at[:, pl.ds(0, 16)], halo.at[1], hl_s.at[0], hl_r.at[1], dev(to, z - 1, x)).start()

        @pl.when(k < WIN - 1)
        def _():
            remote(ref.at[:, pl.ds(CELLS - 16, 16)], halo.at[0], hl_s.at[1], hl_r.at[0], dev(to, z + 1, x)).start()

    def edges_sent(ref):
        @pl.when(k > 0)
        def _():
            arrived(ref.at[:, pl.ds(0, 16)], hl_s.at[0])

        @pl.when(k < WIN - 1)
        def _():
            arrived(ref.at[:, pl.ds(CELLS - 16, 16)], hl_s.at[1])

    @pl.when(k == 0)
    def _():
        halo[0] = jnp.zeros((FR, 16, C), BF16)

    @pl.when(k == WIN - 1)
    def _():
        halo[1] = jnp.zeros((FR, 16, C), BF16)

    def post(src, dst, ssem, rsem, to):
        @pl.when(to != z)
        def _():
            remote(src, dst, ssem, rsem, dev(seg, to, x)).start()

        @pl.when(to == z)
        def _():
            pltpu.make_async_copy(src, dst, rsem).start()

    def posted(src, ssem, to):
        @pl.when(to != z)
        def _():
            arrived(src, ssem)

    low, high = clips.at[:, :, pl.ds(0, 16)], clips.at[:, :, pl.ds(48, 16)]
    goes_up = jnp.logical_and(k == 0, m > 0)
    goes_down = jnp.logical_and(k == WIN - 1, m < WIN - 1)

    @pl.when(first)
    def _():
        regroup(clips, xin, cg_s, cg_r)
        for i in range(MB):
            @pl.when(goes_up)
            def _():
                post(low.at[i], halo.at[1], sc_s.at[16 + i], hl_r.at[1], i * WIN + m - 1)

            @pl.when(goes_down)
            def _():
                post(high.at[i], halo.at[0], sc_s.at[16 + i], hl_r.at[0], i * WIN + m + 1)

        for i in range(MB):
            here = lengths[i]
            masks = [jnp.where(f < here, 1.0, 0.0).astype(F32) for f in range(FR)]
            st_clip[i, 0], st_clip[i, 1] = stats_of(clips.at[i], 8, masks, (here * 64).astype(F32))
            for kk in range(WIN):
                post(st_clip.at[i], st_in.at[z], sc_s.at[i * WIN + kk], sc_r.at[z], i * WIN + kk)

        regroup_recv(xin, cg_r)
        for j in range(ZS):
            arrived(st_in.at[j], sc_r.at[j])
        combine([(st_in[j, 0], st_in[j, 1]) for j in range(ZS)], (length * 64).astype(F32))

    @pl.when(seg > 1)
    def _():
        regroup(cot, cotz, ct_s, ct_r)

    @pl.when(seg > 0)
    def _():
        for h in range(2):
            arrived(xin.at[:, pl.ds(h * 128, 128)], rl_r.at[h])
        for kk in range(WIN):
            arrived(st_in.at[kk], st_r.at[kk])
        combine([(st_in[kk, 0], st_in[kk, 1]) for kk in range(WIN)], n_dev)

    @pl.when(k > 0)
    def _():
        arrived(halo.at[0], hl_r.at[0])

    @pl.when(k < WIN - 1)
    def _():
        arrived(halo.at[1], hl_r.at[1])

    mean = norm[0]
    scale = norm[1] * gain[...]
    offset = jnp.broadcast_to(shift[...], (8, C))
    col = lax.broadcasted_iota(jnp.int32, (1, 8, C), 1)

    def act(v):
        v = (v - mean[None]) * scale[None] + offset[None]
        return v / (1.0 + jnp.exp(-v))

    def put(row, n, per_frame):
        for fp in range(2):
            pair = [per_frame[2 * fp], per_frame[2 * fp + 1]]
            for d in range(3):
                if d == 0:
                    out = [jnp.where(col == 0, 0.0, pltpu.roll(h.reshape(n * 8, C), 1, 0).reshape(n, 8, C)) for h in pair]
                elif d == 2:
                    out = [jnp.where(col == 7, 0.0, pltpu.roll(h.reshape(n * 8, C), n * 8 - 1, 0).reshape(n, 8, C)) for h in pair]
                else:
                    out = pair
                hs[d, pl.ds(row, n), fp] = jnp.concatenate(out, axis=1).astype(BF16)

    top_here, bottom_here = k > 0, k < WIN - 1
    put(0, 1, [jnp.where(top_here, act(halo[0, f, 8:16].astype(F32).reshape(1, 8, C)), 0.0) for f in range(FR)])
    put(ROWS + 1, 1, [jnp.where(bottom_here, act(halo[1, f, 0:8].astype(F32).reshape(1, 8, C)), 0.0) for f in range(FR)])

    def norm_step(j, c):
        put(8 * j + 1, 8, [
            act(xin[f, pl.ds(pl.multiple_of(j * 64, 64), 64)].astype(F32).reshape(8, 8, C)) for f in range(FR)])
        return c

    lax.fori_loop(0, ROWS // 8, norm_step, 0)

    for cp in w_copies:
        cp.wait()

    factor = 1.0 / math.sqrt(MB * XS * FR * 128 * 8)

    def gradient():
        regroup_recv(cotz, ct_r)

        def rhs_step(j, c):
            cut = pl.ds(pl.multiple_of(j * 64, 64), 64)
            cs = [cotz[f, cut].astype(F32).reshape(8, 8, C) * mask[f] for f in range(FR)]
            zero = jnp.zeros((8, 8, C), F32)
            two = cs[0] + cs[1]
            cols = [
                [[two + cs[2], cs[3]], [zero, zero]],
                [[two, cs[2]], [cs[3], zero]],
                [[cs[0], cs[1]], [cs[2], cs[3]]],
            ]
            for a in range(3):
                for fp in range(2):
                    rhs[pl.ds(8 * j, 8), fp, :, a * C:(a + 1) * C] = jnp.concatenate(cols[a][fp], axis=1).astype(BF16)
            return c

        lax.fori_loop(0, ROWS // 8, rhs_step, 0)
        for b in range(CH):
            lhs = jnp.concatenate([hs[d, b:b + ROWS].reshape(ROWS * 32, C) for d in range(3)], axis=1)
            acc = lax.dot_general(
                lhs, rhs[...].reshape(ROWS * 32, 3 * C), (((0,), (0,)), ((), ())), preferred_element_type=F32)
            for a in range(3):
                block = (acc[:, a * C:(a + 1) * C] * factor).astype(BF16)
                for q in range(XS):
                    part[b, q, 3 * a:3 * a + 3] = block[96 * q:96 * q + 96].reshape(3, PR, C)
            for o in (2, 1, 3):
                to = lax.rem(x + o, XS)
                remote(part.at[b, to], xr.at[b, o - 1], xs_s.at[b, o - 1], xs_r.at[b, o - 1],
                       dev(seg, z, to)).start()

    @pl.when(last)
    def _():
        gradient()

    bias_row = bias[...].reshape(1, 1, C)
    half = ROWS // 2
    for h in range(2):
        def taps(fp):
            return jnp.concatenate(
                [hs[d, pl.ds(h * half + b, half), fp].reshape(half * 16, C) for b in range(3) for d in range(3)], axis=1)

        p01 = jnp.dot(taps(0), wcat[...], preferred_element_type=F32).reshape(half, 2, 8, 3 * C)
        p23 = jnp.dot(taps(1), wcat[:, C:], preferred_element_type=F32).reshape(half, 2, 8, 2 * C)
        a0, a1, a2 = slice(0, C), slice(C, 2 * C), slice(2 * C, 3 * C)
        early = p01[:, 0, :, a0] + p01[:, 0, :, a1]
        outs = [
            early + p01[:, 0, :, a2],
            early + p01[:, 1, :, a2],
            p01[:, 0, :, a0] + p01[:, 1, :, a1] + p23[:, 0, :, a1],
            p01[:, 1, :, a0] + p23[:, 0, :, a0] + p23[:, 1, :, a1],
        ]
        for f in range(FR):
            v = xin[f, h * 128:(h + 1) * 128].astype(F32).reshape(half, 8, C)
            out = (v + outs[f] + bias_row) * mask[f]
            xout[f, h * 128:(h + 1) * 128] = out.reshape(128, C).astype(BF16)

        @pl.when(jnp.logical_not(last))
        def _():
            part_h = (slice(None), pl.ds(h * 128, 128))
            remote(xout.at[part_h], xin.at[part_h], rl_s.at[h], rl_r.at[h], dev(nxt, z, x)).start()

    @pl.when(jnp.logical_not(last))
    def _():
        send_edges(xout, nxt)
        st_out[0], st_out[1] = stats_of(xout, ROWS, mask, n_dev)
        for kk in range(WIN):
            remote(st_out, st_in.at[k], st_s.at[kk], st_r.at[k], dev(nxt, m * WIN + kk, x)).start()

    def send_stash():
        for j in range(WIN):
            to = k * WIN + j
            src = xout.at[:, pl.ds(j * 64, 64)]

            @pl.when(to != z)
            def _():
                remote(src, stash.at[m], ss_s.at[j], ss_r.at[m], dev(seg, to, x)).start()

            @pl.when(to == z)
            def _():
                pltpu.make_async_copy(src, stash.at[m], ss_r.at[m]).start()

    @pl.when(jnp.logical_and(seg % 2 == 1, jnp.logical_not(last)))
    def _():
        pl.semaphore_signal(go, inc=1, device_id=dev(seg - 1, z, x), device_id_type=MESH)

    @pl.when(first)
    def _():
        pl.semaphore_wait(go, 1)

    @pl.when(seg <= 1)
    def _():
        regroup(cot, cotz, ct_s, ct_r)

    @pl.when(seg == SEGS - 2)
    def _():
        send_stash()

    @pl.when(jnp.logical_not(last))
    def _():
        gradient()

    order = (8, 7, 9, 6, 10, 5, 11, 4, 12, 3, 13, 2, 14, 1, 15)

    def piece(c, zz):
        return lax.rem(zz + 2 * ZS - PC * c, ZS)

    @pl.when(jnp.logical_and(seg % 2 == 0, jnp.logical_and(seg > 0, seg < SEGS - 2)))
    def _():
        pl.semaphore_wait(go, 1)

    for c in range(CH):
        for o in (1, 3, 2):
            arrived(xr.at[c, o - 1], xs_r.at[c, o - 1])
        for p in range(PC):
            v = part[c, x, p].astype(F32)
            for o in range(3):
                v = v + xr[c, o, p].astype(F32)
            zs[c, p] = v.astype(BF16)
        for o in order:
            to = lax.rem(z + o, ZS)
            p_to = piece(c, to)

            @pl.when(p_to < PC)
            def _():
                remote(zs.at[c, p_to], zr.at[c, o - 1], zs_s.at[c, o - 1], zs_r.at[c, o - 1], dev(seg, to, x)).start()

    @pl.when(jnp.logical_and(seg != SEGS - 2, jnp.logical_not(last)))
    def _():
        send_stash()

    for c in range(CH):
        mine = piece(c, z)

        @pl.when(mine < PC)
        def _():
            v = zs[c, mine].astype(F32)
            for o in order[::-1]:
                arrived(zr.at[c, o - 1], zs_r.at[c, o - 1])
                v = v + zr[c, o - 1].astype(F32)
            kept = grad.at[mine // 3, c, 3 * x + mine % 3]
            kept[...] = v.astype(BF16)
            for o in order:
                remote(kept, kept, ag_s.at[c, o - 1], ag_r.at[c, o - 1], dev(seg, lax.rem(z + o, ZS), x)).start()

    @pl.when(last)
    def _():
        send_stash()

    for c in range(CH):
        for o in order[::-1]:
            p_src = piece(c, lax.rem(z + ZS - o, ZS))

            @pl.when(p_src < PC)
            def _():
                arrived(zr.at[c, o - 1], ag_r.at[c, o - 1])

        quarter = grad.at[:, c, pl.ds(3 * x, 3)]
        for o in (2, 1, 3):
            remote(quarter, quarter, xg_s.at[c, o - 1], xg_r.at[c, o - 1], dev(seg, z, lax.rem(x + o, XS))).start()

    for j in range(MB):
        arrived(stash.at[j], ss_r.at[j])
    for j in range(WIN):
        @pl.when(k * WIN + j != z)
        def _():
            arrived(xout.at[:, pl.ds(j * 64, 64)], ss_s.at[j])

    regroup_sent(cot, ct_s)

    @pl.when(jnp.logical_not(last))
    def _():
        for h in range(2):
            arrived(xout.at[:, pl.ds(h * 128, 128)], rl_s.at[h])
        for kk in range(WIN):
            arrived(st_out, st_s.at[kk])
        edges_sent(xout)

    @pl.when(first)
    def _():
        regroup_sent(clips, cg_s)
        for i in range(MB):
            for kk in range(WIN):
                posted(st_clip.at[i], sc_s.at[i * WIN + kk], i * WIN + kk)

            @pl.when(goes_up)
            def _():
                posted(low.at[i], sc_s.at[16 + i], i * WIN + m - 1)

            @pl.when(goes_down)
            def _():
                posted(high.at[i], sc_s.at[16 + i], i * WIN + m + 1)

    for c in range(CH):
        for o in range(1, XS):
            arrived(xr.at[c, o - 1], xs_s.at[c, o - 1])
        for o in range(1, ZS):
            @pl.when(piece(c, lax.rem(z + o, ZS)) < PC)
            def _():
                arrived(zr.at[c, o - 1], zs_s.at[c, o - 1])

        @pl.when(piece(c, z) < PC)
        def _():
            for o in range(1, ZS):
                arrived(zr.at[c, o - 1], ag_s.at[c, o - 1])

    for c in range(CH):
        for o in range(1, XS):
            arrived(grad.at[:, c, pl.ds(3 * lax.rem(x + XS - o, XS), 3)], xg_r.at[c, o - 1])
            arrived(xr.at[c, o - 1], xg_s.at[c, o - 1])


def per_device(clips, lengths, conv_weight, norm_gain, norm_shift, conv_bias, cotangent):
    vmem, anyspace = pltpu.VMEM, pl.ANY
    dma = pltpu.SemaphoreType.DMA
    stash, grad = pl.pallas_call(
        kernel,
        out_shape=(
            jax.ShapeDtypeStruct((MB, FR, 64, C), BF16),
            jax.ShapeDtypeStruct((3, CH, 12, PR, C), BF16),
        ),
        in_specs=[pl.BlockSpec(memory_space=anyspace)] * 7,
        out_specs=(pl.BlockSpec(memory_space=vmem), pl.BlockSpec(memory_space=vmem)),
        scratch_shapes=[
            vmem((MB, FR, 64, C), BF16),
            pltpu.SMEM((MB,), jnp.int32),
            vmem((1, C), F32), vmem((1, C), F32), vmem((1, C), F32),
            vmem((FR, CELLS, C), BF16),
            vmem((FR, CELLS, C), BF16),
            vmem((2, FR, 16, C), BF16),
            vmem((9 * C, 3 * C), BF16),
            vmem((3, ROWS + 2, 2, 16, C), BF16),
            vmem((FR, CELLS, C), BF16),
            vmem((ROWS, 2, 16, 3 * C), BF16),
            vmem((CH, XS, PC, PR, C), BF16),
            vmem((CH, XS - 1, PC, PR, C), BF16),
            vmem((CH, PC, PR, C), BF16),
            vmem((CH, ZS - 1, PR, C), BF16),
            vmem((2, 8, C), F32),
            vmem((ZS, 2, 8, C), F32),
            vmem((MB, 2, 8, C), F32),
            vmem((2, 8, C), F32),
            pltpu.SemaphoreType.REGULAR,
            dma((5,)),
            dma((3,)),
            dma((4,)), dma((4,)), dma((4,)), dma((4,)), dma((4,)), dma((4,)),
            dma((2,)), dma((2,)), dma((2,)), dma((2,)), dma((4,)), dma((4,)),
            dma((20,)), dma((16,)),
            dma((3, 3)), dma((3, 3)), dma((3, 15)), dma((3, 15)), dma((3, 15)), dma((3, 15)), dma((3, 3)), dma((3, 3)),
        ],
        compiler_params=pltpu.CompilerParams(
            collective_id=0, has_side_effects=True, vmem_limit_bytes=63 * 2**20),
        cost_estimate=pl.CostEstimate(flops=2 * 10**9, bytes_accessed=4 * 10**6, transcendentals=10**6),
    )(
        clips.reshape(MB, FR, 64, C), lengths.reshape(MB), conv_weight[0], norm_gain, norm_shift, conv_bias,
        cotangent.reshape(MB, FR, 64, C))
    grads = grad.reshape(27 * C, C).astype(F32)
    return stash.reshape(1, MB, 1, FR, 8, 8, C), grads[None]


def solution(mesh):
    in_specs = (
        P(None, "dp", None, "rows", None, None),
        P(None, "dp"),
        P("segment", None, None),
        P("segment", None),
        P("segment", None),
        P("segment", None),
        P("segment", None, "dp", None, "rows", None, None),
    )
    out_specs = (P("segment", None, "dp", None, "rows", None, None), P("segment", None, None))
    return jax.shard_map(per_device, mesh=mesh, in_specs=in_specs, out_specs=out_specs, check_vma=False)
```

```python
import math

import jax
import jax.numpy as jnp
from jax import lax
from jax.experimental import pallas as pl
from jax.experimental.pallas import tpu as pltpu
from jax.sharding import PartitionSpec as P

MESH = pl.DeviceIdType.MESH
EPS = 1e-06
SEGS, ZS, XS, MB, FR, C = 8, 16, 4, 4, 4, 128
WIN = 4
ROWS = 32
CELLS = ROWS * 8
CH, PC, PR = 3, 9, 32
F32, BF16 = jnp.float32, jnp.bfloat16


def group_sum(v):
    lane = lax.broadcasted_iota(jnp.int32, v.shape, 1)
    v = v + jnp.where(lane % 2 == 0, pltpu.roll(v, 127, 1), pltpu.roll(v, 1, 1))
    return v + jnp.where(lane % 4 < 2, pltpu.roll(v, 126, 1), pltpu.roll(v, 2, 1))


def kernel(clips_any, lengths_any, w, gain_any, shift_any, bias_any, cot, stash, grad,
           clips, lengths, gain, shift, bias,
           xin, xout, halo, wcat, hs, cotz, rhs, part, xr, zs, zr, st_out, st_in, st_clip, norm, go,
           in_sem, w_sem, cg_s, cg_r, ct_s, ct_r, ss_s, ss_r, rl_s, rl_r, hl_s, hl_r, st_s, st_r,
           sc_s, sc_r,
           xs_s, xs_r, zs_s, zs_r, ag_s, ag_r, xg_s, xg_r):
    seg = lax.axis_index("segment")
    z = lax.axis_index("rows")
    x = lax.axis_index("dp")
    m = z // WIN
    k = z % WIN
    nxt = lax.rem(seg + 1, SEGS)
    prv = lax.rem(seg + SEGS - 1, SEGS)
    first = seg == 0
    last = seg == SEGS - 1

    def dev(s, zz, xx):
        return {"segment": s, "rows": zz, "dp": xx}

    def remote(src, dst, ssem, rsem, target):
        return pltpu.make_async_remote_copy(
            src_ref=src, dst_ref=dst, send_sem=ssem, recv_sem=rsem, device_id=target, device_id_type=MESH)

    def arrived(ref, sem):
        pltpu.make_async_copy(ref, ref, sem).wait()

    in_copies = [
        pltpu.make_async_copy(src, dst, in_sem.at[i])
        for i, (src, dst) in enumerate([
            (clips_any, clips), (lengths_any, lengths), (gain_any, gain), (shift_any, shift), (bias_any, bias)])
    ]
    for cp in in_copies:
        cp.start()

    w_copies = [
        pltpu.make_async_copy(w.at[pl.ds(a * 9 * C, 9 * C)], wcat.at[:, pl.ds(a * C, C)], w_sem.at[a])
        for a in range(3)
    ]
    for cp in w_copies:
        cp.start()

    bar = pltpu.get_barrier_semaphore()

    def greet(target):
        pl.semaphore_signal(bar, inc=1, device_id=target, device_id_type=MESH)

    for o in range(1, ZS):
        greet(dev(seg, lax.rem(z + o, ZS), x))
    for o in range(1, XS):
        greet(dev(seg, z, lax.rem(x + o, XS)))
    for kk in range(WIN):
        greet(dev(nxt, m * WIN + kk, x))
        greet(dev(prv, m * WIN + kk, x))
    for cp in in_copies:
        cp.wait()
    pl.semaphore_wait(bar, ZS - 1 + XS - 1 + 2 * WIN)

    def regroup(src, dst, ssem, rsem):
        for i in range(MB):
            to = i * WIN + m
            here = dst.at[:, pl.ds(pl.multiple_of(k * 64, 64), 64)]

            @pl.when(to != z)
            def _():
                remote(src.at[i], here, ssem.at[i], rsem.at[k], dev(seg, to, x)).start()

            @pl.when(to == z)
            def _():
                pltpu.make_async_copy(src.at[i], here, rsem.at[k]).start()

    def regroup_recv(dst, rsem):
        for j in range(WIN):
            arrived(dst.at[:, pl.ds(j * 64, 64)], rsem.at[j])

    def regroup_sent(src, ssem):
        for i in range(MB):
            @pl.when(i * WIN + m != z)
            def _():
                arrived(src.at[i], ssem.at[i])

    length = lengths[m]
    mask = [jnp.where(f < length, 1.0, 0.0).astype(F32) for f in range(FR)]
    n_dev = (length * CELLS).astype(F32)

    def stats_of(ref, rows, masks, n):
        def over(fn):
            total = jnp.zeros((8, C), F32)
            for f in range(FR):
                total = total + jnp.sum(fn(ref[f].astype(F32).reshape(rows, 8, C)), axis=0) * masks[f]
            return jnp.broadcast_to(jnp.sum(total, axis=0, keepdims=True), (8, C))

        sums = over(lambda v: v)
        mean = (sums / n)[None]
        return sums, over(lambda v: (v - mean) * (v - mean))

    def combine(parts, n):
        count = n * (4.0 * len(parts))
        total = parts[0][0]
        for sums, _ in parts[1:]:
            total = total + sums
        mean = group_sum(total) / count
        spread = jnp.zeros((8, C), F32)
        for sums, squares in parts:
            off = sums / n - mean
            spread = spread + squares + n * (off * off)
        norm[0] = mean
        norm[1] = lax.rsqrt(group_sum(spread) / count + EPS)

    def send_edges(ref, to):
        @pl.when(k > 0)
        def _():
            remote(ref.at[:, pl.ds(0, 16)], halo.at[1], hl_s.at[0], hl_r.at[1], dev(to, z - 1, x)).start()

        @pl.when(k < WIN - 1)
        def _():
            remote(ref.at[:, pl.ds(CELLS - 16, 16)], halo.at[0], hl_s.at[1], hl_r.at[0], dev(to, z + 1, x)).start()

    def edges_sent(ref):
        @pl.when(k > 0)
        def _():
            arrived(ref.at[:, pl.ds(0, 16)], hl_s.at[0])

        @pl.when(k < WIN - 1)
        def _():
            arrived(ref.at[:, pl.ds(CELLS - 16, 16)], hl_s.at[1])

    @pl.when(k == 0)
    def _():
        halo[0] = jnp.zeros((FR, 16, C), BF16)

    @pl.when(k == WIN - 1)
    def _():
        halo[1] = jnp.zeros((FR, 16, C), BF16)

    def post(src, dst, ssem, rsem, to):
        @pl.when(to != z)
        def _():
            remote(src, dst, ssem, rsem, dev(seg, to, x)).start()

        @pl.when(to == z)
        def _():
            pltpu.make_async_copy(src, dst, rsem).start()

    def posted(src, ssem, to):
        @pl.when(to != z)
        def _():
            arrived(src, ssem)

    low, high = clips.at[:, :, pl.ds(0, 16)], clips.at[:, :, pl.ds(48, 16)]
    goes_up = jnp.logical_and(k == 0, m > 0)
    goes_down = jnp.logical_and(k == WIN - 1, m < WIN - 1)

    @pl.when(first)
    def _():
        regroup(clips, xin, cg_s, cg_r)
        for i in range(MB):
            @pl.when(goes_up)
            def _():
                post(low.at[i], halo.at[1], sc_s.at[16 + i], hl_r.at[1], i * WIN + m - 1)

            @pl.when(goes_down)
            def _():
                post(high.at[i], halo.at[0], sc_s.at[16 + i], hl_r.at[0], i * WIN + m + 1)

        for i in range(MB):
            here = lengths[i]
            masks = [jnp.where(f < here, 1.0, 0.0).astype(F32) for f in range(FR)]
            st_clip[i, 0], st_clip[i, 1] = stats_of(clips.at[i], 8, masks, (here * 64).astype(F32))
            for kk in range(WIN):
                post(st_clip.at[i], st_in.at[z], sc_s.at[i * WIN + kk], sc_r.at[z], i * WIN + kk)

        regroup_recv(xin, cg_r)
        for j in range(ZS):
            arrived(st_in.at[j], sc_r.at[j])
        combine([(st_in[j, 0], st_in[j, 1]) for j in range(ZS)], (length * 64).astype(F32))

    @pl.when(seg > 1)
    def _():
        regroup(cot, cotz, ct_s, ct_r)

    def prepare():
        regroup_recv(cotz, ct_r)

        def rhs_step(j, c):
            cut = pl.ds(pl.multiple_of(j * 64, 64), 64)
            cs = [cotz[f, cut].astype(F32).reshape(8, 8, C) * mask[f] for f in range(FR)]
            zero = jnp.zeros((8, 8, C), F32)
            two = cs[0] + cs[1]
            cols = [
                [[two + cs[2], cs[3]], [zero, zero]],
                [[two, cs[2]], [cs[3], zero]],
                [[cs[0], cs[1]], [cs[2], cs[3]]],
            ]
            for a in range(3):
                for fp in range(2):
                    rhs[pl.ds(8 * j, 8), fp, :, a * C:(a + 1) * C] = jnp.concatenate(cols[a][fp], axis=1).astype(BF16)
            return c

        lax.fori_loop(0, ROWS // 8, rhs_step, 0)

    @pl.when(seg > 1)
    def _():
        prepare()

    @pl.when(seg > 0)
    def _():
        for h in range(2):
            arrived(xin.at[:, pl.ds(h * 128, 128)], rl_r.at[h])
        for kk in range(WIN):
            arrived(st_in.at[kk], st_r.at[kk])
        combine([(st_in[kk, 0], st_in[kk, 1]) for kk in range(WIN)], n_dev)

    @pl.when(k > 0)
    def _():
        arrived(halo.at[0], hl_r.at[0])

    @pl.when(k < WIN - 1)
    def _():
        arrived(halo.at[1], hl_r.at[1])

    mean = norm[0]
    scale = norm[1] * gain[...]
    offset = jnp.broadcast_to(shift[...], (8, C))
    col = lax.broadcasted_iota(jnp.int32, (1, 8, C), 1)

    def act(v):
        v = (v - mean[None]) * scale[None] + offset[None]
        return v / (1.0 + jnp.exp(-v))

    def put(row, n, per_frame):
        for fp in range(2):
            pair = [per_frame[2 * fp], per_frame[2 * fp + 1]]
            for d in range(3):
                if d == 0:
                    out = [jnp.where(col == 0, 0.0, pltpu.roll(h.reshape(n * 8, C), 1, 0).reshape(n, 8, C)) for h in pair]
                elif d == 2:
                    out = [jnp.where(col == 7, 0.0, pltpu.roll(h.reshape(n * 8, C), n * 8 - 1, 0).reshape(n, 8, C)) for h in pair]
                else:
                    out = pair
                hs[d, pl.ds(row, n), fp] = jnp.concatenate(out, axis=1).astype(BF16)

    top_here, bottom_here = k > 0, k < WIN - 1
    put(0, 1, [jnp.where(top_here, act(halo[0, f, 8:16].astype(F32).reshape(1, 8, C)), 0.0) for f in range(FR)])
    put(ROWS + 1, 1, [jnp.where(bottom_here, act(halo[1, f, 0:8].astype(F32).reshape(1, 8, C)), 0.0) for f in range(FR)])

    def norm_step(j, c):
        put(8 * j + 1, 8, [
            act(xin[f, pl.ds(pl.multiple_of(j * 64, 64), 64)].astype(F32).reshape(8, 8, C)) for f in range(FR)])
        return c

    lax.fori_loop(0, ROWS // 8, norm_step, 0)

    for cp in w_copies:
        cp.wait()

    factor = 1.0 / math.sqrt(MB * XS * FR * 128 * 8)

    def gradient():
        @pl.when(seg <= 1)
        def _():
            prepare()

        for b in range(CH):
            lhs = jnp.concatenate([hs[d, b:b + ROWS].reshape(ROWS * 32, C) for d in range(3)], axis=1)
            acc = lax.dot_general(
                lhs, rhs[...].reshape(ROWS * 32, 3 * C), (((0,), (0,)), ((), ())), preferred_element_type=F32)
            for a in range(3):
                block = (acc[:, a * C:(a + 1) * C] * factor).astype(BF16)
                for q in range(XS):
                    part[b, q, 3 * a:3 * a + 3] = block[96 * q:96 * q + 96].reshape(3, PR, C)
            for o in (2, 1, 3):
                to = lax.rem(x + o, XS)
                remote(part.at[b, to], xr.at[b, o - 1], xs_s.at[b, o - 1], xs_r.at[b, o - 1],
                       dev(seg, z, to)).start()

    @pl.when(last)
    def _():
        gradient()

    bias_row = bias[...].reshape(1, 1, C)
    half = ROWS // 2
    for h in range(2):
        def taps(fp):
            return jnp.concatenate(
                [hs[d, pl.ds(h * half + b, half), fp].reshape(half * 16, C) for b in range(3) for d in range(3)], axis=1)

        p01 = jnp.dot(taps(0), wcat[...], preferred_element_type=F32).reshape(half, 2, 8, 3 * C)
        p23 = jnp.dot(taps(1), wcat[:, C:], preferred_element_type=F32).reshape(half, 2, 8, 2 * C)
        a0, a1, a2 = slice(0, C), slice(C, 2 * C), slice(2 * C, 3 * C)
        early = p01[:, 0, :, a0] + p01[:, 0, :, a1]
        outs = [
            early + p01[:, 0, :, a2],
            early + p01[:, 1, :, a2],
            p01[:, 0, :, a0] + p01[:, 1, :, a1] + p23[:, 0, :, a1],
            p01[:, 1, :, a0] + p23[:, 0, :, a0] + p23[:, 1, :, a1],
        ]
        for f in range(FR):
            v = xin[f, h * 128:(h + 1) * 128].astype(F32).reshape(half, 8, C)
            out = (v + outs[f] + bias_row) * mask[f]
            xout[f, h * 128:(h + 1) * 128] = out.reshape(128, C).astype(BF16)

        @pl.when(jnp.logical_not(last))
        def _():
            part_h = (slice(None), pl.ds(h * 128, 128))
            remote(xout.at[part_h], xin.at[part_h], rl_s.at[h], rl_r.at[h], dev(nxt, z, x)).start()

    @pl.when(jnp.logical_not(last))
    def _():
        send_edges(xout, nxt)
        st_out[0], st_out[1] = stats_of(xout, ROWS, mask, n_dev)
        for kk in range(WIN):
            remote(st_out, st_in.at[k], st_s.at[kk], st_r.at[k], dev(nxt, m * WIN + kk, x)).start()

    def send_stash():
        for j in range(WIN):
            to = k * WIN + j
            src = xout.at[:, pl.ds(j * 64, 64)]

            @pl.when(to != z)
            def _():
                remote(src, stash.at[m], ss_s.at[j], ss_r.at[m], dev(seg, to, x)).start()

            @pl.when(to == z)
            def _():
                pltpu.make_async_copy(src, stash.at[m], ss_r.at[m]).start()

    @pl.when(jnp.logical_and(seg % 2 == 1, jnp.logical_not(last)))
    def _():
        pl.semaphore_signal(go, inc=1, device_id=dev(seg - 1, z, x), device_id_type=MESH)

    @pl.when(first)
    def _():
        pl.semaphore_wait(go, 1)

    @pl.when(seg <= 1)
    def _():
        regroup(cot, cotz, ct_s, ct_r)

    @pl.when(seg == SEGS - 2)
    def _():
        send_stash()

    @pl.when(jnp.logical_not(last))
    def _():
        gradient()

    order = (8, 7, 9, 6, 10, 5, 11, 4, 12, 3, 13, 2, 14, 1, 15)

    def piece(c, zz):
        return lax.rem(zz + 2 * ZS - PC * c, ZS)

    @pl.when(jnp.logical_and(seg % 2 == 0, jnp.logical_and(seg > 0, seg < SEGS - 2)))
    def _():
        pl.semaphore_wait(go, 1)

    for c in range(CH):
        for o in (1, 3, 2):
            arrived(xr.at[c, o - 1], xs_r.at[c, o - 1])
        for p in range(PC):
            v = part[c, x, p].astype(F32)
            for o in range(3):
                v = v + xr[c, o, p].astype(F32)
            zs[c, p] = v.astype(BF16)
        for o in order:
            to = lax.rem(z + o, ZS)
            p_to = piece(c, to)

            @pl.when(p_to < PC)
            def _():
                remote(zs.at[c, p_to], zr.at[c, o - 1], zs_s.at[c, o - 1], zs_r.at[c, o - 1], dev(seg, to, x)).start()

    @pl.when(jnp.logical_and(seg != SEGS - 2, jnp.logical_not(last)))
    def _():
        send_stash()

    for c in range(CH):
        mine = piece(c, z)

        @pl.when(mine < PC)
        def _():
            v = zs[c, mine].astype(F32)
            for o in order[::-1]:
                arrived(zr.at[c, o - 1], zs_r.at[c, o - 1])
                v = v + zr[c, o - 1].astype(F32)
            kept = grad.at[mine // 3, c, 3 * x + mine % 3]
            kept[...] = v.astype(BF16)
            for o in order:
                remote(kept, kept, ag_s.at[c, o - 1], ag_r.at[c, o - 1], dev(seg, lax.rem(z + o, ZS), x)).start()

    @pl.when(last)
    def _():
        send_stash()

    for c in range(CH):
        for o in order[::-1]:
            p_src = piece(c, lax.rem(z + ZS - o, ZS))

            @pl.when(p_src < PC)
            def _():
                arrived(zr.at[c, o - 1], ag_r.at[c, o - 1])

        quarter = grad.at[:, c, pl.ds(3 * x, 3)]
        for o in (2, 1, 3):
            remote(quarter, quarter, xg_s.at[c, o - 1], xg_r.at[c, o - 1], dev(seg, z, lax.rem(x + o, XS))).start()

    for j in range(MB):
        arrived(stash.at[j], ss_r.at[j])
    for j in range(WIN):
        @pl.when(k * WIN + j != z)
        def _():
            arrived(xout.at[:, pl.ds(j * 64, 64)], ss_s.at[j])

    regroup_sent(cot, ct_s)

    @pl.when(jnp.logical_not(last))
    def _():
        for h in range(2):
            arrived(xout.at[:, pl.ds(h * 128, 128)], rl_s.at[h])
        for kk in range(WIN):
            arrived(st_out, st_s.at[kk])
        edges_sent(xout)

    @pl.when(first)
    def _():
        regroup_sent(clips, cg_s)
        for i in range(MB):
            for kk in range(WIN):
                posted(st_clip.at[i], sc_s.at[i * WIN + kk], i * WIN + kk)

            @pl.when(goes_up)
            def _():
                posted(low.at[i], sc_s.at[16 + i], i * WIN + m - 1)

            @pl.when(goes_down)
            def _():
                posted(high.at[i], sc_s.at[16 + i], i * WIN + m + 1)

    for c in range(CH):
        for o in range(1, XS):
            arrived(xr.at[c, o - 1], xs_s.at[c, o - 1])
        for o in range(1, ZS):
            @pl.when(piece(c, lax.rem(z + o, ZS)) < PC)
            def _():
                arrived(zr.at[c, o - 1], zs_s.at[c, o - 1])

        @pl.when(piece(c, z) < PC)
        def _():
            for o in range(1, ZS):
                arrived(zr.at[c, o - 1], ag_s.at[c, o - 1])

    for c in range(CH):
        for o in range(1, XS):
            arrived(grad.at[:, c, pl.ds(3 * lax.rem(x + XS - o, XS), 3)], xg_r.at[c, o - 1])
            arrived(xr.at[c, o - 1], xg_s.at[c, o - 1])


def per_device(clips, lengths, conv_weight, norm_gain, norm_shift, conv_bias, cotangent):
    vmem, anyspace = pltpu.VMEM, pl.ANY
    dma = pltpu.SemaphoreType.DMA
    stash, grad = pl.pallas_call(
        kernel,
        out_shape=(
            jax.ShapeDtypeStruct((MB, FR, 64, C), BF16),
            jax.ShapeDtypeStruct((3, CH, 12, PR, C), BF16),
        ),
        in_specs=[pl.BlockSpec(memory_space=anyspace)] * 7,
        out_specs=(pl.BlockSpec(memory_space=vmem), pl.BlockSpec(memory_space=vmem)),
        scratch_shapes=[
            vmem((MB, FR, 64, C), BF16),
            pltpu.SMEM((MB,), jnp.int32),
            vmem((1, C), F32), vmem((1, C), F32), vmem((1, C), F32),
            vmem((FR, CELLS, C), BF16),
            vmem((FR, CELLS, C), BF16),
            vmem((2, FR, 16, C), BF16),
            vmem((9 * C, 3 * C), BF16),
            vmem((3, ROWS + 2, 2, 16, C), BF16),
            vmem((FR, CELLS, C), BF16),
            vmem((ROWS, 2, 16, 3 * C), BF16),
            vmem((CH, XS, PC, PR, C), BF16),
            vmem((CH, XS - 1, PC, PR, C), BF16),
            vmem((CH, PC, PR, C), BF16),
            vmem((CH, ZS - 1, PR, C), BF16),
            vmem((2, 8, C), F32),
            vmem((ZS, 2, 8, C), F32),
            vmem((MB, 2, 8, C), F32),
            vmem((2, 8, C), F32),
            pltpu.SemaphoreType.REGULAR,
            dma((5,)),
            dma((3,)),
            dma((4,)), dma((4,)), dma((4,)), dma((4,)), dma((4,)), dma((4,)),
            dma((2,)), dma((2,)), dma((2,)), dma((2,)), dma((4,)), dma((4,)),
            dma((20,)), dma((16,)),
            dma((3, 3)), dma((3, 3)), dma((3, 15)), dma((3, 15)), dma((3, 15)), dma((3, 15)), dma((3, 3)), dma((3, 3)),
        ],
        compiler_params=pltpu.CompilerParams(
            collective_id=0, has_side_effects=True, vmem_limit_bytes=63 * 2**20),
        cost_estimate=pl.CostEstimate(flops=2 * 10**9, bytes_accessed=4 * 10**6, transcendentals=10**6),
    )(
        clips.reshape(MB, FR, 64, C), lengths.reshape(MB), conv_weight[0], norm_gain, norm_shift, conv_bias,
        cotangent.reshape(MB, FR, 64, C))
    grads = grad.reshape(27 * C, C).astype(F32)
    return stash.reshape(1, MB, 1, FR, 8, 8, C), grads[None]


def solution(mesh):
    in_specs = (
        P(None, "dp", None, "rows", None, None),
        P(None, "dp"),
        P("segment", None, None),
        P("segment", None),
        P("segment", None),
        P("segment", None),
        P("segment", None, "dp", None, "rows", None, None),
    )
    out_specs = (P("segment", None, "dp", None, "rows", None, None), P("segment", None, None))
    return jax.shard_map(per_device, mesh=mesh, in_specs=in_specs, out_specs=out_specs, check_vma=False)
```
